32 devices in a mesh: grp: 2 (over x), seq: 16 (over z, y, core).
Axes of the slice: x: 2, y: 2, z: 4, core: 2. Of those that a mesh axis runs over, the one named last changes fastest.
Arguments:
- query_in: bfloat16 [4096, 4096], P(('grp', 'seq')), parts along dimension 0, may hold values from -6 to 6
- key_in: bfloat16 [4096, 4096], P(('grp', 'seq')), parts along dimension 0, may hold values from -6 to 6
- value_in: bfloat16 [4096, 4096], P(('grp', 'seq')), parts along dimension 0, may hold values from -6 to 6
- short_filter: float32 [3, 3, 4096], replicated, may hold values from -4 to 4
- residue: float32 [4096, 16], replicated, may hold values from -0.125 to 0.125
- rate: float32 [4096, 16], replicated, may hold values from 0.000390625 to 0.03
- skip: float32 [4096], replicated, may hold values from -5 to 5
Outputs:
- gated: bfloat16 [4096, 4096], P(('grp', 'seq')), parts along dimension 0
The draws below stay inside these ranges and needn't reach their ends.
There are 2 independent parts, one for each index of `grp`. The reference program is written for one: setup_inputs(seed, part) draws one part's arguments, and reference() takes and returns one part's arrays. A program takes and returns all parts, laid end to end along the dimension named above; an argument that names none is the same for every part. Nothing has to cross between parts.
All inputs are finite; a program needn't handle non-finite values.
Results may differ from the reference program's by a relative error of at most 0.0049.
Values may be sent and summed in bfloat16 or wider, within the bound.
No kernel may reach another device: no remote copies, remote signals or barrier semaphores. Data moves between devices by JAX's collectives and lax.ppermute only.
A program may use at most 192 MiB of HBM per device.

```python
import math
import jax
import jax.numpy as jnp

C = 4096
TOK_DEV = 128
SHORT = 3
MODES = 16
TOKENS = 2048


def level_of(own_key, shape, cuts, smallest, top_value):
    def one(position, blocks):
        steps = jax.random.uniform(jax.random.fold_in(jax.random.fold_in(own_key, 6), position), (blocks,), jnp.float32, smallest / len(cuts), top_value / len(cuts))
        return jnp.repeat(jnp.exp(steps), shape[position] // blocks).reshape((-1,) + (1,) * (len(shape) - position - 1))

    gain = one(*cuts[0])
    for cut in cuts[1:]:
        gain = gain * one(*cut)
    return gain


def normal_values(key, shape, spread, limit, shards=(), held_as=jnp.bfloat16):
    level = level_of(key, shape, shards, -0.22, 0.18) if shards else 1.0
    array = jax.random.normal(key, shape, jnp.float32) * spread * level
    return jnp.minimum(jnp.maximum(array, -limit), limit).astype(held_as)


def setup_inputs(seed: int = 0, part: int = 0) -> dict:
    splits = jax.random.split(jax.random.key(seed), 8)
    part_splits = jax.random.split(jax.random.fold_in(splits[7], part), 8)
    return {
        "query_in": normal_values(part_splits[0], (TOKENS, C), 1.0, 6.0, ((0, 16),)),
        "key_in": normal_values(part_splits[1], (TOKENS, C), 1.0, 6.0, ((0, 16),)),
        "value_in": normal_values(part_splits[2], (TOKENS, C), 1.0, 6.0, ((0, 16),)),
        "short_filter": normal_values(splits[3], (3, SHORT, C), 0.6, 4.0, (), jnp.float32),
        "residue": normal_values(splits[4], (C, MODES), (MODES * TOK_DEV) ** -0.5, 0.125, (), jnp.float32),
        "rate": jnp.clip(jnp.exp(jax.random.uniform(splits[5], (C, MODES), jnp.float32, math.log(0.000390625), math.log(0.03))), 0.000390625, 0.03),
        "skip": normal_values(splits[6], (C,), 1.0, 5.0, (), jnp.float32),
    }


def featurize(signal, taps):
    whole = signal.astype(jnp.float32)
    result = taps[0] * whole
    for offset in range(1, taps.shape[0]):
        shifted = jnp.concatenate([jnp.zeros((offset, whole.shape[1]), jnp.float32), whole[:-offset]], axis=0)
        result = result + taps[offset] * shifted
    return result


def reference(query_in, key_in, value_in, short_filter, residue, rate, skip):
    length = query_in.shape[0]
    width = query_in.shape[1]
    query_feat = featurize(query_in, short_filter[0])
    key_feat = featurize(key_in, short_filter[1])
    value_feat = featurize(value_in, short_filter[2])
    mixed = (key_feat * value_feat).astype(jnp.bfloat16)
    span = 2 * TOK_DEV
    steps = jnp.arange(span).astype(jnp.float32)
    fft_len = 1
    while fft_len < length + span:
        fft_len = fft_len * 2
    block = min(256, width)
    pieces = []
    for start in range(0, width, block):
        weights = residue[start:start + block]
        decays = rate[start:start + block]
        filt = jnp.sum(weights[None] * jnp.exp(-decays[None] * steps[:, None, None]), axis=2)
        signal = mixed[:, start:start + block].astype(jnp.float32)
        spectrum = jnp.fft.rfft(signal, n=fft_len, axis=0) * jnp.fft.rfft(filt, n=fft_len, axis=0)
        conv = jnp.fft.irfft(spectrum, n=fft_len, axis=0)[:length]
        conv = conv + skip[start:start + block] * signal
        pieces.append((query_feat[:, start:start + block] * conv).astype(jnp.bfloat16))
    return jnp.concatenate(pieces, axis=1)
```

```python
import functools
import math
from decimal import Decimal, localcontext

import jax
import jax.numpy as jnp
import numpy as np
from jax import lax
from jax.experimental import pallas as pl
from jax.experimental.pallas import tpu as pltpu
from jax.sharding import PartitionSpec as P

RATE_LOW, RATE_HIGH = 0.000390625, 0.03
NODES = 8
TILE = 512


def separable_basis(rows):
    cosines = [math.cos(math.pi * (j + 0.5) / NODES) for j in range(NODES)]
    with localcontext() as context:
        context.prec = 50
        times = [Decimal(str(round((rows - 1) / 2 * (1 - v), 2))) for v in cosines]
        span = RATE_HIGH - RATE_LOW
        rates = [Decimal(str(round(RATE_LOW + span * ((1 - v) / 2) ** 1.3, 6))) for v in cosines]
        table = [
            [(-r * t).exp() for t in times] + [(-r * t).exp() for t in range(rows)] for r in rates
        ]
        for i in range(NODES):
            best = max(range(i, NODES), key=lambda k: abs(table[k][i]))
            table[i], table[best] = table[best], table[i]
            inverse = 1 / table[i][i]
            table[i] = [v * inverse for v in table[i]]
            for k in range(NODES):
                if k != i:
                    factor = table[k][i]
                    table[k] = [a - factor * b for a, b in zip(table[k], table[i])]
        basis = np.array([[float(v) for v in table[i][NODES:]] for i in range(NODES)], np.float64)
    return [float(t) for t in times], basis


def make_tables(rows):
    times, basis = separable_basis(rows)
    place = np.arange(rows)
    delta = place[:, None] - place[None, :]
    wrapped = basis[:, delta % rows]
    lower = np.where(delta[None] >= 0, wrapped, 0.0)
    upper = np.where(delta[None] < 0, wrapped, 0.0)
    pieces = [lower[j] for j in range(NODES)] + [upper[j] for j in range(NODES)]
    pieces += [basis.T, np.zeros((rows, NODES))]
    outputs = np.concatenate(pieces, axis=1).astype(np.float32)
    moments = basis[:, ::-1].astype(np.float32)
    high = moments.astype(jnp.bfloat16)
    low = (moments - high.astype(np.float32)).astype(jnp.bfloat16)
    return times, outputs.astype(jnp.bfloat16), np.concatenate([high, low], axis=0)


def featurize(signal, taps, rim=None):
    whole = signal.astype(jnp.float32)
    row = lax.broadcasted_iota(jnp.int32, whole.shape, 0)
    result = taps[0:1] * whole
    for offset in range(1, taps.shape[0]):
        shifted = pltpu.roll(whole, offset, axis=0)
        for r in range(offset):
            edge = 0.0 if rim is None else rim[rim.shape[0] - offset + r : rim.shape[0] - offset + r + 1]
            shifted = jnp.where(row == r, edge, shifted)
        result = result + taps[offset : offset + 1] * shifted
    return result


def mix_kernel(key_ref, value_ref, taps_ref, mixed_ref):
    kf = featurize(key_ref[...], taps_ref[1])
    vf = featurize(value_ref[...], taps_ref[2])
    mixed_ref[...] = (kf * vf).astype(mixed_ref.dtype)


def coefficient_kernel(times, rows, residue_ref, rate_ref, near_ref, far_ref):
    weights, rates = residue_ref[...], rate_ref[...]
    far_weights = weights * jnp.exp(-rates * float(rows))
    near, far = [], []
    for t in times:
        decay = jnp.exp(-rates * t)
        near.append(jnp.sum(weights * decay, axis=0, keepdims=True))
        far.append(jnp.sum(far_weights * decay, axis=0, keepdims=True))
    keep = (lax.axis_index("seq") >= 2).astype(jnp.float32)
    near_ref[...] = jnp.concatenate(near, axis=0)
    far_ref[...] = jnp.concatenate(far, axis=0) * keep


def edge_kernel(
    times, edge, bounds, key_ref, value_ref, rims_ref, taps_ref, residue_ref, rate_ref, moment_ref,
    mixed_ref, fix_ref, middle_ref, third_ref, fourth_ref,
):
    tile = pl.program_id(0)
    keep = (lax.axis_index("seq") >= 1).astype(jnp.float32)
    rims = rims_ref[...].astype(jnp.float32) * keep
    kf = featurize(key_ref[...], taps_ref[1], rims[edge : 2 * edge])
    vf = featurize(value_ref[...], taps_ref[2], rims[2 * edge : 3 * edge])
    mixed = (kf * vf).astype(jnp.bfloat16)
    mixed_ref[...] = mixed
    fix_ref[...] = mixed[0:8]
    halves = jnp.dot(moment_ref[...], mixed, preferred_element_type=jnp.float32)
    moments = halves[:NODES] + halves[NODES:]
    weights, rates = residue_ref[...], rate_ref[...]
    decays = [jnp.exp(-rates * t) for t in times]
    state = decays[0] * moments[0:1]
    for j in range(1, NODES):
        state = state + decays[j] * moments[j : j + 1]
    state = state * (weights * jnp.exp(-rates))
    middle = [jnp.sum(decays[i] * state, axis=0, keepdims=True) for i in range(NODES)]
    middle_ref[...] = jnp.concatenate(middle, axis=0).astype(middle_ref.dtype)

    @pl.when((tile >= bounds[2]) & (tile < bounds[3]))
    def _():
        third_ref[...] = mixed

    @pl.when(tile >= bounds[3])
    def _():
        fourth_ref[...] = mixed


def finish_kernel(
    edge, fixed, query_ref, mixed_ref, back_ref, fix_ref, middle_ref, near_ref, far_ref, taps_ref, rims_ref,
    skip_ref, table_ref, _, out_ref, stack_ref,
):
    rows = query_ref.shape[0]
    keep = (lax.axis_index("seq") >= 1).astype(jnp.float32)
    mixed = mixed_ref[...].astype(jnp.float32)
    back = back_ref[...].astype(jnp.float32)
    if fixed:
        row = lax.broadcasted_iota(jnp.int32, back.shape, 0)
        back = jnp.where(row == 1, fix_ref[1:2].astype(jnp.float32), back)
    for j in range(NODES):
        stack_ref[j * rows : (j + 1) * rows] = (mixed * near_ref[j : j + 1]).astype(stack_ref.dtype)
        stack_ref[(NODES + j) * rows : (NODES + j + 1) * rows] = (back * far_ref[j : j + 1]).astype(stack_ref.dtype)
    middle = middle_ref[...].astype(jnp.float32) * keep
    middle = jnp.concatenate([middle, jnp.zeros_like(middle)], axis=0)
    stack_ref[2 * NODES * rows : 2 * NODES * rows + 2 * NODES] = middle.astype(stack_ref.dtype)
    conv = jnp.dot(table_ref[...], stack_ref[...], preferred_element_type=jnp.float32)
    conv = conv + skip_ref[...] * mixed
    qf = featurize(query_ref[...], taps_ref[0], rims_ref[0:edge].astype(jnp.float32) * keep)
    out_ref[...] = (qf * conv).astype(out_ref.dtype)


def ring(array, by):
    length = lax.axis_size("seq")
    return lax.ppermute(array, "seq", [(i, (i + by) % length) for i in range(length)])


def params(limit=24):
    return pltpu.CompilerParams(vmem_limit_bytes=limit * 1024 * 1024)


def shards(query_in, key_in, value_in, short_filter, residue, rate, skip):
    rows, width = query_in.shape
    kinds, count, _ = short_filter.shape
    edge = count - 1
    modes = residue.shape[1]
    times, table, moment_table = make_tables(rows)
    table, moment_table = jnp.asarray(table), jnp.asarray(moment_table)
    residue_t, rate_t, skip_row = residue.T, rate.T, skip.reshape(1, width)
    tile = math.gcd(TILE, width // 4)
    tiles = width // tile
    cuts = [0, tiles // 4, tiles // 2, 3 * tiles // 4, tiles]
    spans = [(cuts[i], cuts[i + 1]) for i in range(4)]

    def mixed_part(first, last):
        n = last - first
        return pl.pallas_call(
            mix_kernel,
            grid=(n,),
            in_specs=[pl.BlockSpec((rows, tile), lambda i: (0, first + i))] * 2
            + [pl.BlockSpec((kinds, count, tile), lambda i: (0, 0, first + i))],
            out_specs=pl.BlockSpec((rows, tile), lambda i: (0, i)),
            out_shape=jax.ShapeDtypeStruct((rows, n * tile), jnp.bfloat16),
            compiler_params=params(),
        )(key_in, value_in, short_filter)

    back = [None] * 4
    back[0] = ring(mixed_part(*spans[0]), 2)
    rims = ring(jnp.concatenate([query_in[rows - edge :], key_in[rows - edge :], value_in[rows - edge :]], axis=0), 1)
    back[1] = ring(mixed_part(*spans[1]), 2)

    near, far = pl.pallas_call(
        functools.partial(coefficient_kernel, times, rows),
        grid=(tiles,),
        in_specs=[pl.BlockSpec((modes, tile), lambda i: (0, i))] * 2,
        out_specs=[pl.BlockSpec((NODES, tile), lambda i: (0, i))] * 2,
        out_shape=[jax.ShapeDtypeStruct((NODES, width), jnp.float32)] * 2,
        compiler_params=params(),
    )(residue_t, rate_t)

    column = lambda i: (0, i)
    mixed, fix, middle, third, fourth = pl.pallas_call(
        functools.partial(edge_kernel, times, edge, cuts),
        grid=(tiles,),
        in_specs=[
            pl.BlockSpec((rows, tile), column),
            pl.BlockSpec((rows, tile), column),
            pl.BlockSpec((kinds * edge, tile), column),
            pl.BlockSpec((kinds, count, tile), lambda i: (0, 0, i)),
            pl.BlockSpec((modes, tile), column),
            pl.BlockSpec((modes, tile), column),
            pl.BlockSpec((2 * NODES, rows), lambda i: (0, 0)),
        ],
        out_specs=[
            pl.BlockSpec((rows, tile), column),
            pl.BlockSpec((8, tile), column),
            pl.BlockSpec((NODES, tile), column),
            pl.BlockSpec((rows, tile), lambda i: (0, jnp.clip(i - cuts[2], 0, cuts[3] - cuts[2] - 1))),
            pl.BlockSpec((rows, tile), lambda i: (0, jnp.clip(i - cuts[3], 0, cuts[4] - cuts[3] - 1))),
        ],
        out_shape=[
            jax.ShapeDtypeStruct((rows, width), jnp.bfloat16),
            jax.ShapeDtypeStruct((8, width), jnp.bfloat16),
            jax.ShapeDtypeStruct((NODES, width), jnp.bfloat16),
            jax.ShapeDtypeStruct((rows, (cuts[3] - cuts[2]) * tile), jnp.bfloat16),
            jax.ShapeDtypeStruct((rows, (cuts[4] - cuts[3]) * tile), jnp.bfloat16),
        ],
        compiler_params=params(),
    )(key_in, value_in, rims, short_filter, residue_t, rate_t, moment_table)
    middle = ring(middle, 1)
    fix = ring(fix[:, : cuts[2] * tile], 2)
    back[2] = ring(third, 2)
    back[3] = ring(fourth, 2)

    def finish(part, out):
        first, last = spans[part]
        own = lambda i: (0, first + i)
        fixed = part < 2
        return pl.pallas_call(
            functools.partial(finish_kernel, edge, fixed),
            grid=(last - first,),
            in_specs=[
                pl.BlockSpec((rows, tile), own),
                pl.BlockSpec((rows, tile), own),
                pl.BlockSpec((rows, tile), lambda i: (0, i)),
                pl.BlockSpec((8, tile), own if fixed else (lambda i: (0, 0))),
                pl.BlockSpec((NODES, tile), own),
                pl.BlockSpec((NODES, tile), own),
                pl.BlockSpec((NODES, tile), own),
                pl.BlockSpec((kinds, count, tile), lambda i: (0, 0, first + i)),
                pl.BlockSpec((kinds * edge, tile), own),
                pl.BlockSpec((1, tile), own),
                pl.BlockSpec(table.shape, lambda i: (0, 0)),
                pl.BlockSpec(memory_space=pl.ANY),
            ],
            out_specs=pl.BlockSpec((rows, tile), own),
            out_shape=jax.ShapeDtypeStruct((rows, width), jnp.bfloat16),
            scratch_shapes=[pltpu.VMEM((table.shape[1], tile), jnp.bfloat16)],
            input_output_aliases={11: 0} if out is not None else {},
            compiler_params=params(),
        )(query_in, mixed, back[part], fix, middle, near, far, short_filter, rims, skip_row, table,
          query_in if out is None else out)

    out = None
    for part in range(4):
        out = finish(part, out)
    return out


def solution(mesh):
    return jax.shard_map(
        shards,
        mesh=mesh,
        in_specs=(P(("grp", "seq"), None),) * 3 + (P(),) * 4,
        out_specs=P(("grp", "seq"), None),
        check_vma=False,
    )
```

```python
import functools
import math
from decimal import Decimal, localcontext

import jax
import jax.numpy as jnp
import numpy as np
from jax import lax
from jax.experimental import pallas as pl
from jax.experimental.pallas import tpu as pltpu
from jax.sharding import PartitionSpec as P

RATE_LOW, RATE_HIGH = 0.000390625, 0.03
NODES = 8
OWN_COST = 80000000


def separable_basis(rows):
    cosines = [math.cos(math.pi * (j + 0.5) / NODES) for j in range(NODES)]
    with localcontext() as context:
        context.prec = 50
        times = [Decimal(str(round((rows - 1) / 2 * (1 - v), 2))) for v in cosines]
        span = RATE_HIGH - RATE_LOW
        rates = [Decimal(str(round(RATE_LOW + span * ((1 - v) / 2) ** 1.3, 6))) for v in cosines]
        table = [
            [(-r * t).exp() for t in times] + [(-r * t).exp() for t in range(rows)] for r in rates
        ]
        for i in range(NODES):
            best = max(range(i, NODES), key=lambda k: abs(table[k][i]))
            table[i], table[best] = table[best], table[i]
            inverse = 1 / table[i][i]
            table[i] = [v * inverse for v in table[i]]
            for k in range(NODES):
                if k != i:
                    factor = table[k][i]
                    table[k] = [a - factor * b for a, b in zip(table[k], table[i])]
        basis = np.array([[float(v) for v in table[i][NODES:]] for i in range(NODES)], np.float64)
    return [float(t) for t in times], basis


def make_tables(rows):
    times, basis = separable_basis(rows)
    place = np.arange(rows)
    delta = place[:, None] - place[None, :]
    wrapped = basis[:, delta % rows]
    lower = np.where(delta[None] >= 0, wrapped, 0.0)
    upper = np.where(delta[None] < 0, wrapped, 0.0)
    near = np.concatenate(list(lower) + [basis.T, np.zeros((rows, NODES))], axis=1).astype(np.float32)
    far = np.concatenate(list(upper), axis=1).astype(np.float32)
    moments = basis[:, ::-1].astype(np.float32)
    high = moments.astype(jnp.bfloat16)
    low = (moments - high.astype(np.float32)).astype(jnp.bfloat16)
    return times, near.astype(jnp.bfloat16), far.astype(jnp.bfloat16), np.concatenate([high, low], axis=0)


def shifted(whole, offset, rim):
    rolled = pltpu.roll(whole, offset, axis=0)
    top = rolled[:8]
    row = lax.broadcasted_iota(jnp.int32, top.shape, 0)
    for r in range(offset):
        at = None if rim is None else rim.shape[0] - offset + r
        top = jnp.where(row == r, 0.0 if rim is None else rim[at : at + 1], top)
    return top if whole.shape[0] == 8 else jnp.concatenate([top, rolled[8:]], axis=0)


def featurize(signal, taps, rim=None):
    whole = signal.astype(jnp.float32)
    result = taps[0:1] * whole
    for offset in range(1, taps.shape[0]):
        result = result + taps[offset : offset + 1] * shifted(whole, offset, rim)
    return result


def columns(start, stop, step):
    return [(at, min(at + step, stop)) for at in range(start, stop, step)]


def early_kernel(key_ref, value_ref, taps_ref, mixed_ref, key_vmem, value_vmem, taps_vmem, sems):
    rows, width = mixed_ref.shape
    spans = columns(0, width, 256)
    taps_copy = pltpu.make_async_copy(taps_ref.at[:, :, pl.ds(0, width)], taps_vmem, sems.at[0])
    taps_copy.start()
    copies = []
    for n, (a, b) in enumerate(spans):
        at = pl.ds(a, b - a)
        pair = (
            pltpu.make_async_copy(key_ref.at[:, at], key_vmem.at[:, at], sems.at[1 + 2 * n]),
            pltpu.make_async_copy(value_ref.at[:, at], value_vmem.at[:, at], sems.at[2 + 2 * n]),
        )
        for copy in pair:
            copy.start()
        copies.append(pair)
    taps_copy.wait()
    for (a, b), pair in zip(spans, copies):
        for copy in pair:
            copy.wait()
        kf = featurize(key_vmem[:, a:b], taps_vmem[1, :, a:b])
        vf = featurize(value_vmem[:, a:b], taps_vmem[2, :, a:b])
        mixed_ref[:, a:b] = (kf * vf).astype(mixed_ref.dtype)


def second_kernel(
    start, edge, _, query_ref, key_ref, value_ref, taps_ref, residue_ref, rate_ref, mixed_ref, rims_ref, key_vmem,
    value_vmem, taps_vmem, residue_vmem, rate_vmem, held, sems,
):
    rows, width = mixed_ref.shape
    whole = key_ref.shape[1]
    count = 0

    def copy(source, target):
        nonlocal count
        made = pltpu.make_async_copy(source, target, sems.at[count])
        made.start()
        count += 1
        return made

    taps_copy = copy(taps_ref, taps_vmem)
    spans = columns(start, start + width, 256)
    cut = lambda a, b: [
        copy(ref.at[:, pl.ds(a, b - a)], vmem.at[:, pl.ds(a, b - a)])
        for ref, vmem in ((key_ref, key_vmem), (value_ref, value_vmem))
    ]
    copies = [cut(a, b) for a, b in spans]
    rim_copy = copy(query_ref.at[pl.ds(rows - 8, 8)], held)
    rest = cut(start + width, whole) + cut(0, start)
    rest += [copy(residue_ref, residue_vmem), copy(rate_ref, rate_vmem)]
    taps_copy.wait()
    for (a, b), pair in zip(spans, copies):
        for made in pair:
            made.wait()
        kf = featurize(key_vmem[:, a:b], taps_vmem[1, :, a:b])
        vf = featurize(value_vmem[:, a:b], taps_vmem[2, :, a:b])
        mixed_ref[:, a - start : b - start] = (kf * vf).astype(mixed_ref.dtype)
    rim_copy.wait()
    for made in rest:
        made.wait()
    for n, last in enumerate((held[...], key_vmem[rows - 16 :][8:], value_vmem[rows - 16 :][8:])):
        rims_ref[:, n * whole : (n + 1) * whole] = last[8 - edge :]


def pass_kernel(*refs):
    del refs


def prepare_kernel(
    times, rows, residue_ref, rate_ref, moment_ref, c1, c2, near_ref, far_ref, state_ref, first_ref, second_ref,
    decay_ref, spread_ref,
):
    modes, width = rate_ref.shape
    keep = (lax.axis_index("seq") >= 2).astype(jnp.float32)
    early = c1.shape[1]
    for c, d in columns(0, width, 256):
        weights, rates = residue_ref[:, c:d], rate_ref[:, c:d]
        far_weights = weights * jnp.exp(-rates * float(rows))
        later = weights * jnp.exp(-rates)
        near, far = [], []
        for j, t in enumerate(times):
            decay = jnp.exp(-rates * t)
            near.append(jnp.sum(weights * decay, axis=0, keepdims=True))
            far.append(jnp.sum(far_weights * decay, axis=0, keepdims=True))
            decay_ref[j * modes : (j + 1) * modes, c:d] = decay
            spread_ref[j * modes : (j + 1) * modes, c:d] = later * decay
        near_ref[:, c:d] = jnp.concatenate(near, axis=0)
        far_ref[:, c:d] = jnp.concatenate(far, axis=0) * keep
        if c < state_ref.shape[1]:
            part = c1[:, c:d] if c < early else c2[:, c - early : d - early]
            state_ref[:, c:d] = modal_state(moment_ref, part, decay_ref, c, d)
            first_ref[:, c:d] = jnp.exp(-rates * float(rows - 1))
            second_ref[:, c:d] = jnp.exp(-rates * float(rows - 2))


def modal_state(moment_ref, mixed, decay_ref, c, d):
    halves = jnp.dot(moment_ref[...], mixed, preferred_element_type=jnp.float32)
    moments = halves[:NODES] + halves[NODES:]
    modes = decay_ref.shape[0] // NODES
    state = decay_ref[0:modes, c:d] * moments[0:1]
    for j in range(1, NODES):
        state = state + decay_ref[j * modes : (j + 1) * modes, c:d] * moments[j : j + 1]
    return state


def edge_kernel(
    edge, _, key_ref, value_ref, rims_ref, taps_ref, moment_ref, c1, c2, state_ref, first_ref, second_ref, decay_ref,
    spread_ref, c3, c4, head_ref, fix_ref, middle_ref,
):
    width = key_ref.shape[1]
    early = c1.shape[1] + c2.shape[1]
    modes = state_ref.shape[0]
    keep = (lax.axis_index("seq") >= 1).astype(jnp.float32)
    offset = 0
    for chunk in (c1, c2, c3, c4):
        for a, b in columns(0, chunk.shape[1], 256):
            c, d = offset + a, offset + b
            key_rim = rims_ref[:, width + c : width + d].astype(jnp.float32) * keep
            value_rim = rims_ref[:, 2 * width + c : 2 * width + d].astype(jnp.float32) * keep
            if c < early:
                kf = featurize(key_ref[0:16, c:d].astype(jnp.float32)[:8], taps_ref[1, :, c:d], key_rim)
                vf = featurize(value_ref[0:16, c:d].astype(jnp.float32)[:8], taps_ref[2, :, c:d], value_rim)
                head = (kf * vf).astype(jnp.bfloat16)
                head_ref[:, c:d] = head
                fix_ref[:, c:d] = head[:edge]
                delta = head.astype(jnp.float32) - chunk[0:16, a:b].astype(jnp.float32)[:8]
                state = state_ref[:, c:d] + first_ref[:, c:d] * delta[0:1] + second_ref[:, c:d] * delta[1:2]
            else:
                kf = featurize(key_ref[:, c:d], taps_ref[1, :, c:d], key_rim)
                vf = featurize(value_ref[:, c:d], taps_ref[2, :, c:d], value_rim)
                mixed = (kf * vf).astype(jnp.bfloat16)
                chunk[:, a:b] = mixed
                state = modal_state(moment_ref, mixed, decay_ref, c, d)
            middle = [
                jnp.sum(spread_ref[i * modes : (i + 1) * modes, c:d] * state, axis=0, keepdims=True)
                for i in range(NODES)
            ]
            middle_ref[:, c:d] = jnp.concatenate(middle, axis=0).astype(middle_ref.dtype)
        offset = offset + chunk.shape[1]


def own_kernel(
    edge, query_ref, c1, c2, c3, c4, head_ref, near_ref, taps_ref, rims_ref, skip_ref, middle_ref, table_ref, part_ref,
    gate_ref, stack_ref,
):
    rows, _ = query_ref.shape
    keep = (lax.axis_index("seq") >= 1).astype(jnp.float32)
    offset = 0
    for chunk in (c1, c2, c3, c4):
        for a, b in columns(0, chunk.shape[1], stack_ref.shape[1]):
            c, d = offset + a, offset + b
            mixed = chunk[:, a:b].astype(jnp.float32)
            if c < head_ref.shape[1]:
                mixed = jnp.concatenate([head_ref[:, c:d].astype(jnp.float32), mixed[8:]], axis=0)
            for j in range(NODES):
                stack_ref[j * rows : (j + 1) * rows, : b - a] = (mixed * near_ref[j : j + 1, c:d]).astype(stack_ref.dtype)
            middle = middle_ref[:, c:d].astype(jnp.float32) * keep
            middle = jnp.concatenate([middle, jnp.zeros_like(middle)], axis=0)
            stack_ref[NODES * rows : NODES * rows + 2 * NODES, : b - a] = middle.astype(stack_ref.dtype)
            conv = jnp.dot(table_ref[...], stack_ref[:, : b - a], preferred_element_type=jnp.float32)
            part_ref[:, c:d] = conv + skip_ref[:, c:d] * mixed
            rim = rims_ref[:, c:d].astype(jnp.float32) * keep
            gate_ref[:, c:d] = featurize(query_ref[:, c:d], taps_ref[0, :, c:d], rim)
        offset = offset + chunk.shape[1]


def finish_kernel(
    offset, fixed, back_ref, fix_ref, far_ref, part_ref, gate_ref, table_ref, _, out_ref, stack_ref,
    stage_ref, sems,
):
    rows, width = back_ref.shape
    copies = []
    for n, (a, b) in enumerate(columns(0, width, stack_ref.shape[1])):
        c, d = offset + a, offset + b
        back = back_ref[:, a:b].astype(jnp.float32)
        if fixed:
            top = back[:8]
            row = lax.broadcasted_iota(jnp.int32, top.shape, 0)
            top = jnp.where(row == 1, fix_ref[1:2, c:d].astype(jnp.float32), top)
            back = jnp.concatenate([top, back[8:]], axis=0)
        for j in range(NODES):
            stack_ref[j * rows : (j + 1) * rows, : b - a] = (back * far_ref[j : j + 1, c:d]).astype(stack_ref.dtype)
        conv = jnp.dot(table_ref[...], stack_ref[:, : b - a], preferred_element_type=jnp.float32)
        stage_ref[:, a:b] = (gate_ref[:, c:d] * (part_ref[:, c:d] + conv)).astype(stage_ref.dtype)
        copies.append(pltpu.make_async_copy(stage_ref.at[:, pl.ds(a, b - a)], out_ref.at[:, pl.ds(c, b - a)], sems.at[n]))
        copies[-1].start()
    for copy in copies:
        copy.wait()


def ring(array, by, closed=True):
    length = lax.axis_size("seq")
    return lax.ppermute(
        array, "seq", [(i, (i + by) % length) for i in range(length) if closed or i + by < length]
    )


def shards(query_in, key_in, value_in, short_filter, residue, rate, skip):
    rows, width = query_in.shape
    kinds, count, _ = short_filter.shape
    edge = count - 1
    modes = residue.shape[1]
    times, near_table, far_table, moment_table = make_tables(rows)
    near_table, far_table, moment_table = (jnp.asarray(t) for t in (near_table, far_table, moment_table))
    residue_t, rate_t, skip_row = residue.T, rate.T, skip.reshape(1, width)
    unit = width // 32
    cuts = [0, 8 * unit, 18 * unit, 25 * unit, 32 * unit]
    sizes = [cuts[i + 1] - cuts[i] for i in range(4)]
    bf16, f32 = jnp.bfloat16, jnp.float32
    vmem, hbm, anywhere = (pl.BlockSpec(memory_space=m) for m in (pltpu.VMEM, pltpu.HBM, pl.ANY))

    def call(body, ins, outs, operands, scratch=(), limit=40, cost=1, **kw):
        return pl.pallas_call(
            body,
            in_specs=ins,
            out_specs=[o[2] if len(o) > 2 else vmem for o in outs],
            out_shape=[jax.ShapeDtypeStruct(o[0], o[1]) for o in outs],
            scratch_shapes=list(scratch),
            compiler_params=pltpu.CompilerParams(vmem_limit_bytes=limit * 1024 * 1024),
            cost_estimate=pl.CostEstimate(flops=cost, bytes_accessed=cost, transcendentals=0),
            **kw,
        )(*(pltpu.with_memory_space_constraint(x, pltpu.HBM) if i is hbm else x for i, x in zip(ins, operands)))

    back = [None] * 4
    (c1,) = call(
        early_kernel,
        [hbm] * 3,
        [((rows, sizes[0]), bf16)],
        (key_in, value_in, short_filter),
        [
            pltpu.VMEM((rows, sizes[0]), bf16),
            pltpu.VMEM((rows, sizes[0]), bf16),
            pltpu.VMEM((kinds, count, sizes[0]), f32),
            pltpu.SemaphoreType.DMA((1 + 2 * len(columns(0, sizes[0], 256)),)),
        ],
    )
    back[0] = ring(c1, 2)
    c2, rims, key_v, value_v, taps_v, residue_v, rate_v = call(
        functools.partial(second_kernel, cuts[1], edge),
        [anywhere] + [hbm] * 6,
        [
            ((rows, sizes[1]), bf16),
            ((edge, kinds * width), bf16),
            ((rows, width), bf16),
            ((rows, width), bf16),
            (short_filter.shape, f32),
            ((modes, width), f32),
            ((modes, width), f32),
        ],
        (c1, query_in, key_in, value_in, short_filter, residue_t, rate_t),
        [pltpu.VMEM((8, width), bf16), pltpu.SemaphoreType.DMA((8 + 2 * len(columns(0, sizes[1], 256)),))],
    )
    rims_in = ring(rims, 1)
    back[1] = ring(c2, 2)
    near, far, *states = call(
        functools.partial(prepare_kernel, times, rows),
        [vmem] * 5,
        [((NODES, width), f32)] * 2 + [((modes, cuts[2]), f32)] * 3 + [((NODES * modes, width), f32)] * 2,
        (residue_v, rate_v, moment_table, c1, c2),
    )
    c3, c4, head, fix, middle = call(
        functools.partial(edge_kernel, edge),
        [anywhere] + [vmem] * 12,
        [
            ((rows, sizes[2]), bf16),
            ((rows, sizes[3]), bf16),
            ((8, cuts[2]), bf16),
            ((edge, cuts[2]), bf16),
            ((NODES, width), bf16),
        ],
        (back[0], key_v, value_v, rims_in, taps_v, moment_table, c1, c2, *states),
    )
    fix = ring(fix, 2)
    middle_in = ring(middle, 1)
    back[2] = ring(c3, 2)
    (c4,) = call(
        pass_kernel, [anywhere] * 3, [((rows, sizes[3]), bf16, anywhere)], (fix, middle_in, c4), input_output_aliases={2: 0}
    )
    back[3] = ring(c4, 2, closed=False)

    tile = 512
    part, gate = call(
        functools.partial(own_kernel, edge),
        [vmem] * 12,
        [((rows, width), f32)] * 2,
        (query_in, c1, c2, c3, c4, head, near, taps_v, rims_in, skip_row, middle_in, near_table),
        [pltpu.VMEM((near_table.shape[1], tile), bf16)],
        cost=OWN_COST,
    )
    out = None
    for i in range(4):
        (out,) = call(
            functools.partial(finish_kernel, cuts[i], i < 2),
            [vmem] * 6 + [anywhere],
            [((rows, width), bf16, hbm)],
            (back[i], fix, far, part, gate, far_table, query_in if out is None else out),
            [
                pltpu.VMEM((far_table.shape[1], tile), bf16),
                pltpu.VMEM((rows, sizes[i]), bf16),
                pltpu.SemaphoreType.DMA((len(columns(0, sizes[i], tile)),)),
            ],
            input_output_aliases={} if out is None else {6: 0},
        )
    return out


def solution(mesh):
    return jax.shard_map(
        shards,
        mesh=mesh,
        in_specs=(P(("grp", "seq"), None),) * 3 + (P(),) * 4,
        out_specs=P(("grp", "seq"), None),
        check_vma=False,
    )
```

```python
import functools
import math
from decimal import Decimal, localcontext

import jax
import jax.numpy as jnp
import numpy as np
from jax import lax
from jax.experimental import pallas as pl
from jax.experimental.pallas import tpu as pltpu
from jax.sharding import PartitionSpec as P

RATE_LOW, RATE_HIGH = 0.000390625, 0.03
NODES = 8
LAST_TILE = 256


def separable_basis(rows):
    cosines = [math.cos(math.pi * (j + 0.5) / NODES) for j in range(NODES)]
    with localcontext() as context:
        context.prec = 50
        times = [Decimal(str(round((rows - 1) / 2 * (1 - v), 2))) for v in cosines]
        span = RATE_HIGH - RATE_LOW
        rates = [Decimal(str(round(RATE_LOW + span * ((1 - v) / 2) ** 1.3, 6))) for v in cosines]
        table = [
            [(-r * t).exp() for t in times] + [(-r * t).exp() for t in range(rows)] for r in rates
        ]
        for i in range(NODES):
            best = max(range(i, NODES), key=lambda k: abs(table[k][i]))
            table[i], table[best] = table[best], table[i]
            inverse = 1 / table[i][i]
            table[i] = [v * inverse for v in table[i]]
            for k in range(NODES):
                if k != i:
                    factor = table[k][i]
                    table[k] = [a - factor * b for a, b in zip(table[k], table[i])]
        basis = np.array([[float(v) for v in table[i][NODES:]] for i in range(NODES)], np.float64)
    return [float(t) for t in times], basis


def make_tables(rows):
    times, basis = separable_basis(rows)
    place = np.arange(rows)
    delta = place[:, None] - place[None, :]
    wrapped = basis[:, delta % rows]
    lower = np.where(delta[None] >= 0, wrapped, 0.0)
    upper = np.where(delta[None] < 0, wrapped, 0.0)
    near = np.concatenate(list(lower), axis=1).astype(np.float32)
    far = np.concatenate(list(upper) + [basis.T, np.zeros((rows, NODES))], axis=1).astype(np.float32)
    moments = basis[:, ::-1].astype(np.float32)
    high = moments.astype(jnp.bfloat16)
    low = (moments - high.astype(np.float32)).astype(jnp.bfloat16)
    last = [float(v) for v in basis[:, rows - 1]]
    return times, last, near.astype(jnp.bfloat16), far.astype(jnp.bfloat16), np.concatenate([high, low], axis=0)


def shifted(whole, offset, rim):
    rolled = pltpu.roll(whole, offset, axis=0)
    top = rolled[:8]
    row = lax.broadcasted_iota(jnp.int32, top.shape, 0)
    for r in range(offset):
        at = None if rim is None else rim.shape[0] - offset + r
        top = jnp.where(row == r, 0.0 if rim is None else rim[at : at + 1], top)
    return top if whole.shape[0] == 8 else jnp.concatenate([top, rolled[8:]], axis=0)


def featurize(signal, taps, rim=None):
    whole = signal.astype(jnp.float32)
    result = taps[0:1] * whole
    for offset in range(1, taps.shape[0]):
        result = result + taps[offset : offset + 1] * shifted(whole, offset, rim)
    return result


def columns(start, stop, step):
    return [(at, min(at + step, stop)) for at in range(start, stop, step)]


def early_kernel(key_ref, value_ref, taps_ref, mixed_ref, key_vmem, value_vmem, taps_vmem, sems):
    rows, width = mixed_ref.shape
    spans = columns(0, width, 256)
    taps_copy = pltpu.make_async_copy(taps_ref.at[:, :, pl.ds(0, width)], taps_vmem, sems.at[0])
    taps_copy.start()
    copies = []
    for n, (a, b) in enumerate(spans):
        at = pl.ds(a, b - a)
        pair = (
            pltpu.make_async_copy(key_ref.at[:, at], key_vmem.at[:, at], sems.at[1 + 2 * n]),
            pltpu.make_async_copy(value_ref.at[:, at], value_vmem.at[:, at], sems.at[2 + 2 * n]),
        )
        for copy in pair:
            copy.start()
        copies.append(pair)
    taps_copy.wait()
    for (a, b), pair in zip(spans, copies):
        for copy in pair:
            copy.wait()
        kf = featurize(key_vmem[:, a:b], taps_vmem[1, :, a:b])
        vf = featurize(value_vmem[:, a:b], taps_vmem[2, :, a:b])
        mixed_ref[:, a:b] = (kf * vf).astype(mixed_ref.dtype)


def second_kernel(
    start, edge, _, query_ref, key_ref, value_ref, taps_ref, residue_ref, rate_ref, mixed_ref, rims_ref, taps_vmem,
    residue_vmem, rate_vmem, key_vmem, value_vmem, held, sems,
):
    rows, width = mixed_ref.shape
    whole = key_ref.shape[1]
    count = 0

    def copy(source, target):
        nonlocal count
        made = pltpu.make_async_copy(source, target, sems.at[count])
        made.start()
        count += 1
        return made

    taps_copy = copy(taps_ref, taps_vmem)
    spans = columns(0, width, 256)
    copies = [
        [
            copy(ref.at[:, pl.ds(start + a, b - a)], vmem.at[:, pl.ds(a, b - a)])
            for ref, vmem in ((key_ref, key_vmem), (value_ref, value_vmem))
        ]
        for a, b in spans
    ]
    rest = [copy(ref.at[pl.ds(rows - 8, 8)], held.at[n]) for n, ref in enumerate((query_ref, key_ref, value_ref))]
    rest += [copy(residue_ref, residue_vmem), copy(rate_ref, rate_vmem)]
    taps_copy.wait()
    for (a, b), pair in zip(spans, copies):
        for made in pair:
            made.wait()
        kf = featurize(key_vmem[:, a:b], taps_vmem[1, :, start + a : start + b])
        vf = featurize(value_vmem[:, a:b], taps_vmem[2, :, start + a : start + b])
        mixed_ref[:, a:b] = (kf * vf).astype(mixed_ref.dtype)
    for made in rest:
        made.wait()
    for n in range(held.shape[0]):
        rims_ref[:, n * whole : (n + 1) * whole] = held[n][8 - edge :]


def pass_kernel(*refs):
    del refs


def prepare_kernel(
    times, rows, key_ref, value_ref, residue_ref, rate_ref, moment_ref, c1, c2, near_ref, far_ref, state_ref, first_ref,
    second_ref, decay_ref, spread_ref, key_vmem, value_vmem, sems,
):
    modes, width = rate_ref.shape
    keep = (lax.axis_index("seq") >= 2).astype(jnp.float32)
    early, late = c1.shape[1], state_ref.shape[1]
    copies = []
    for ref, vmem in ((key_ref, key_vmem), (value_ref, value_vmem)):
        for tall, a, b in ((rows, late, width), (16, 0, late)):
            at = (pl.ds(0, tall), pl.ds(a, b - a))
            copies.append(pltpu.make_async_copy(ref.at[at], vmem.at[at], sems.at[len(copies)]))
            copies[-1].start()
    for c, d in columns(0, early, 256) + columns(early, late, 256) + columns(late, width, 256):
        weights, rates = residue_ref[:, c:d], rate_ref[:, c:d]
        far_weights = weights * jnp.exp(-rates * float(rows))
        later = weights * jnp.exp(-rates)
        near, far = [], []
        for j, t in enumerate(times):
            decay = jnp.exp(-rates * t)
            near.append(jnp.sum(weights * decay, axis=0, keepdims=True))
            far.append(jnp.sum(far_weights * decay, axis=0, keepdims=True))
            decay_ref[j * modes : (j + 1) * modes, c:d] = decay
            spread_ref[j * modes : (j + 1) * modes, c:d] = later * decay
        near_ref[:, c:d] = jnp.concatenate(near, axis=0)
        far_ref[:, c:d] = jnp.concatenate(far, axis=0) * keep
        if c < late:
            part = c1[:, c:d] if c < early else c2[:, c - early : d - early]
            state_ref[:, c:d] = modal_state(moment_ref, part, decay_ref, c, d)
            first_ref[:, c:d] = jnp.exp(-rates * float(rows - 1))
            second_ref[:, c:d] = jnp.exp(-rates * float(rows - 2))
    for copy in copies:
        copy.wait()


def modal_state(moment_ref, mixed, decay_ref, c, d):
    halves = jnp.dot(moment_ref[...], mixed, preferred_element_type=jnp.float32)
    moments = halves[:NODES] + halves[NODES:]
    modes = decay_ref.shape[0] // NODES
    state = decay_ref[0:modes, c:d] * moments[0:1]
    for j in range(1, NODES):
        state = state + decay_ref[j * modes : (j + 1) * modes, c:d] * moments[j : j + 1]
    return state


def edge_kernel(
    key_ref, value_ref, rims_ref, taps_ref, moment_ref, c1, c2, state_ref, first_ref, second_ref, decay_ref,
    spread_ref, head_ref, middle_ref, *late,
):
    width = key_ref.shape[1]
    early = c1.shape[1] + c2.shape[1]
    modes = state_ref.shape[0]
    keep = (lax.axis_index("seq") >= 1).astype(jnp.float32)
    offset = 0
    for chunk in (c1, c2, *late):
        for a, b in columns(0, chunk.shape[1], 256):
            c, d = offset + a, offset + b
            key_rim = rims_ref[:, width + c : width + d].astype(jnp.float32) * keep
            value_rim = rims_ref[:, 2 * width + c : 2 * width + d].astype(jnp.float32) * keep
            if c < early:
                kf = featurize(key_ref[0:16, c:d].astype(jnp.float32)[:8], taps_ref[1, :, c:d], key_rim)
                vf = featurize(value_ref[0:16, c:d].astype(jnp.float32)[:8], taps_ref[2, :, c:d], value_rim)
                head = (kf * vf).astype(jnp.bfloat16)
                delta = head.astype(jnp.float32) - chunk[0:16, a:b].astype(jnp.float32)[:8]
                state = state_ref[:, c:d] + first_ref[:, c:d] * delta[0:1] + second_ref[:, c:d] * delta[1:2]
            else:
                kf = featurize(key_ref[:, c:d], taps_ref[1, :, c:d], key_rim)
                vf = featurize(value_ref[:, c:d], taps_ref[2, :, c:d], value_rim)
                mixed = (kf * vf).astype(jnp.bfloat16)
                head = mixed[:8]
                state = modal_state(moment_ref, mixed, decay_ref, c, d)
                slot = c - early
                if slot < early:
                    second = head_ref[:, slot : slot + b - a].astype(jnp.float32)[1:2]
                    whole = (kf * vf)[:16]
                    row = lax.broadcasted_iota(jnp.int32, whole.shape, 0)
                    chunk[0:16, a:b] = jnp.where(row == 0, second, whole).astype(jnp.bfloat16)
                    chunk[16:, a:b] = mixed[16:]
                else:
                    chunk[:, a:b] = mixed
            head_ref[:, c:d] = head
            middle = [
                jnp.sum(spread_ref[i * modes : (i + 1) * modes, c:d] * state, axis=0, keepdims=True)
                for i in range(NODES)
            ]
            middle_ref[:, c:d] = jnp.concatenate(middle, axis=0).astype(middle_ref.dtype)
        offset = offset + chunk.shape[1]


def own_kernel(edge, start, query_ref, head_ref, near_ref, taps_ref, rims_ref, skip_ref, table_ref, *refs):
    *chunks, part_ref, gate_ref, stack_ref = refs
    rows, _ = query_ref.shape
    keep = (lax.axis_index("seq") >= 1).astype(jnp.float32)
    offset = start
    for chunk in chunks:
        for a, b in columns(0, chunk.shape[1], stack_ref.shape[1]):
            c, d = offset + a, offset + b
            mixed = chunk[:, a:b].astype(jnp.float32)
            mixed = jnp.concatenate([head_ref[:, c:d].astype(jnp.float32), mixed[8:]], axis=0)
            for j in range(NODES):
                stack_ref[j * rows : (j + 1) * rows, : b - a] = (mixed * near_ref[j : j + 1, c:d]).astype(stack_ref.dtype)
            conv = jnp.dot(table_ref[...], stack_ref[:, : b - a], preferred_element_type=jnp.float32)
            part_ref[:, c - start : d - start] = conv + skip_ref[:, c:d] * mixed
            rim = rims_ref[:, c:d].astype(jnp.float32) * keep
            gate_ref[:, c - start : d - start] = featurize(query_ref[:, c:d], taps_ref[0, :, c:d], rim)
        offset = offset + chunk.shape[1]


def finish_kernel(offset, base, slots, last, middle_ref, far_ref, part_ref, gate_ref, table_ref, *refs):
    keep = (lax.axis_index("seq") >= 1).astype(jnp.float32)
    if slots is None:
        _, *backs, out_ref, pre_ref, stack_ref, stage_ref, sems = refs
    else:
        pre_ref, _, *backs, out_ref, stack_ref, stage_ref, repair_ref, sems = refs
    copies = []

    def write(source, rows, c, d):
        copies.append(pltpu.make_async_copy(source, out_ref.at[pl.ds(0, rows), pl.ds(c, d - c)], sems.at[len(copies)]))
        copies[-1].start()

    at = 0
    for back_ref in backs:
        rows, width = back_ref.shape
        for a, b in columns(0, width, stack_ref.shape[1]):
            c, d = offset + at + a, offset + at + b
            back = back_ref[:, a:b].astype(jnp.float32)
            for j in range(NODES):
                stack_ref[j * rows : (j + 1) * rows, : b - a] = (back * far_ref[j : j + 1, c:d]).astype(stack_ref.dtype)
            middle = middle_ref[:, c:d].astype(jnp.float32) * keep
            middle = jnp.concatenate([middle, jnp.zeros_like(middle)], axis=0)
            stack_ref[NODES * rows : NODES * rows + 2 * NODES, : b - a] = middle.astype(stack_ref.dtype)
            conv = jnp.dot(table_ref[...], stack_ref[:, : b - a], preferred_element_type=jnp.float32)
            total = part_ref[:, c - base : d - base] + conv
            gate = gate_ref[:, c - base : d - base]
            stage_ref[:, at + a : at + b] = (gate * total).astype(stage_ref.dtype)
            write(stage_ref.at[:, pl.ds(at + a, b - a)], rows, c, d)
            if slots is None:
                pre_ref[0:16, c:d] = total[:16]
                pre_ref[16:32, c:d] = gate[:16]
                pre_ref[32:40, c:d] = back[:8]
        at = at + width
    start = 0
    for (first, stop), back_ref in zip(slots or (), backs):
        for c, d in columns(first, stop, 512):
            end = far_ref[0:1, c:d] * last[0]
            for j in range(1, NODES):
                end = end + far_ref[j : j + 1, c:d] * last[j]
            right = back_ref[0:16, c - first : d - first].astype(jnp.float32)[0:1]
            total = pre_ref[0:16, c:d]
            row = lax.broadcasted_iota(jnp.int32, total.shape, 0)
            total = jnp.where(row == 0, total + end * (right - pre_ref[33:34, c:d]), total)
            repair_ref[:, start + c - first : start + d - first] = (pre_ref[16:32, c:d] * total).astype(repair_ref.dtype)
        if stop > first:
            write(repair_ref.at[:, pl.ds(start, stop - first)], 16, first, stop)
        start = start + stop - first
    for copy in copies:
        copy.wait()


def ring(array, by, closed=True):
    length = lax.axis_size("seq")
    return lax.ppermute(
        array, "seq", [(i, (i + by) % length) for i in range(length) if closed or i + by < length]
    )


def shards(query_in, key_in, value_in, short_filter, residue, rate, skip):
    rows, width = query_in.shape
    kinds, count, _ = short_filter.shape
    edge = count - 1
    modes = residue.shape[1]
    times, last, near_table, far_table, moment_table = make_tables(rows)
    near_table, far_table, moment_table = (jnp.asarray(t) for t in (near_table, far_table, moment_table))
    residue_t, rate_t, skip_row = residue.T, rate.T, skip.reshape(1, width)
    unit = width // 32
    cuts = [0, 7 * unit, 15 * unit, 21 * unit, 27 * unit, 32 * unit]
    count_chunks = len(cuts) - 1
    sizes = [cuts[i + 1] - cuts[i] for i in range(count_chunks)]
    bf16, f32 = jnp.bfloat16, jnp.float32
    vmem, hbm, anywhere = (pl.BlockSpec(memory_space=m) for m in (pltpu.VMEM, pltpu.HBM, pl.ANY))

    def call(body, ins, outs, operands, scratch=(), limit=40, cost=1, **kw):
        return pl.pallas_call(
            body,
            in_specs=ins,
            out_specs=[o[2] if len(o) > 2 else vmem for o in outs],
            out_shape=[jax.ShapeDtypeStruct(o[0], o[1]) for o in outs],
            scratch_shapes=list(scratch),
            compiler_params=pltpu.CompilerParams(vmem_limit_bytes=limit * 1024 * 1024),
            cost_estimate=pl.CostEstimate(flops=cost, bytes_accessed=cost, transcendentals=0),
            **kw,
        )(*(pltpu.with_memory_space_constraint(x, pltpu.HBM) if i is hbm else x for i, x in zip(ins, operands)))

    back = [None] * count_chunks
    (c1,) = call(
        early_kernel,
        [hbm] * 3,
        [((rows, sizes[0]), bf16)],
        (key_in, value_in, short_filter),
        [
            pltpu.VMEM((rows, sizes[0]), bf16),
            pltpu.VMEM((rows, sizes[0]), bf16),
            pltpu.VMEM((kinds, count, sizes[0]), f32),
            pltpu.SemaphoreType.DMA((1 + 2 * len(columns(0, sizes[0], 256)),)),
        ],
    )
    back[0] = ring(c1, 2)
    c2, rims, taps_v, residue_v, rate_v = call(
        functools.partial(second_kernel, cuts[1], edge),
        [anywhere] + [hbm] * 6,
        [
            ((rows, sizes[1]), bf16),
            ((edge, kinds * width), bf16),
            (short_filter.shape, f32),
            ((modes, width), f32),
            ((modes, width), f32),
        ],
        (c1, query_in, key_in, value_in, short_filter, residue_t, rate_t),
        [
            pltpu.VMEM((rows, sizes[1]), bf16),
            pltpu.VMEM((rows, sizes[1]), bf16),
            pltpu.VMEM((kinds, 8, width), bf16),
            pltpu.SemaphoreType.DMA((3 + kinds + 2 * len(columns(0, sizes[1], 256)),)),
        ],
    )
    rims_in = ring(rims, 1)
    back[1] = ring(c2, 2)
    near, far, *states, key_v, value_v = call(
        functools.partial(prepare_kernel, times, rows),
        [hbm] * 2 + [vmem] * 5,
        [((NODES, width), f32)] * 2
        + [((modes, cuts[2]), f32)] * 3
        + [((NODES * modes, width), f32)] * 2
        + [((rows, width), bf16)] * 2,
        (key_in, value_in, residue_v, rate_v, moment_table, c1, c2),
        [pltpu.SemaphoreType.DMA((4,))],
    )
    late = range(2, count_chunks)
    head, middle, *chunks = call(
        edge_kernel,
        [vmem] * 12,
        [((8, width), bf16), ((NODES, width), bf16)] + [((rows, sizes[i]), bf16) for i in late],
        (key_v, value_v, rims_in, taps_v, moment_table, c1, c2, *states),
    )
    middle_in = ring(middle, 1)
    for i in late[:-1]:
        back[i] = ring(chunks[i - 2], 2, closed=i < late[-2])

    tile = 512

    def own(first, stop, some):
        return call(
            functools.partial(own_kernel, edge, cuts[first]),
            [vmem] * (7 + len(some)),
            [((rows, cuts[stop] - cuts[first]), f32)] * 2,
            (query_in, head, near, taps_v, rims_in, skip_row, near_table, *some),
            [pltpu.VMEM((near_table.shape[1], tile), bf16)],
        )

    early_own = own(0, 2, (c1, c2))
    (final,) = call(
        pass_kernel,
        [anywhere] * 4,
        [((rows, sizes[-1]), bf16, anywhere)],
        (middle_in, early_own[0], back[0], chunks[-1]),
        input_output_aliases={3: 0},
    )
    back[-1] = ring(final, 2, closed=False)
    late_own = own(2, count_chunks, chunks)

    def finish(first, stop, out, pre):
        some = range(first, stop)
        size = cuts[stop] - cuts[first]
        step = tile if stop < count_chunks else LAST_TILE
        pieces = sum(len(columns(0, sizes[i], step)) for i in some)
        scratch = [pltpu.VMEM((far_table.shape[1], step), bf16), pltpu.VMEM((rows, size), bf16)]
        slots = None
        if out is not None:
            slots = [(min(cuts[i] - cuts[2], cuts[2]), min(cuts[i + 1] - cuts[2], cuts[2])) for i in some]
            scratch.append(pltpu.VMEM((16, max(sum(b - a for a, b in slots), unit)), bf16))
        scratch.append(pltpu.SemaphoreType.DMA((pieces + len(some),)))
        return call(
            functools.partial(finish_kernel, cuts[first], cuts[0 if out is None else 2], slots, last),
            [vmem] * 5 + ([anywhere] if out is None else [vmem, anywhere]) + [vmem] * len(some),
            [((rows, width), bf16, anywhere)] + ([((40, cuts[2]), f32)] if out is None else []),
            (middle_in, far, *(early_own if out is None else late_own), far_table)
            + ((late_own[0],) if out is None else (pre, out))
            + tuple(back[i] for i in some),
            scratch,
            input_output_aliases={} if out is None else {6: 0},
        )

    out, pre = finish(0, 2, None, None)
    (out,) = finish(2, count_chunks - 1, out, pre)
    (out,) = finish(count_chunks - 1, count_chunks, out, pre)
    return out


def solution(mesh):
    return jax.shard_map(
        shards,
        mesh=mesh,
        in_specs=(P(("grp", "seq"), None),) * 3 + (P(),) * 4,
        out_specs=P(("grp", "seq"), None),
        check_vma=False,
    )
```

```python
import functools
import math
from decimal import Decimal, localcontext

import jax
import jax.numpy as jnp
import numpy as np
from jax import lax
from jax.experimental import pallas as pl
from jax.experimental.pallas import tpu as pltpu
from jax.sharding import PartitionSpec as P

RATE_LOW, RATE_HIGH = 0.000390625, 0.03
NODES = 7
PADDED = 8
LAST_TILE = 256


def separable_basis(rows):
    cosines = [math.cos(math.pi * (j + 0.5) / NODES) for j in range(NODES)]
    with localcontext() as context:
        context.prec = 50
        times = [Decimal(str(round((rows - 1) / 2 * (1 - v), 2))) for v in cosines]
        span = RATE_HIGH - RATE_LOW
        rates = [Decimal(str(round(RATE_LOW + span * ((1 - v) / 2) ** 1.3, 6))) for v in cosines]
        table = [
            [(-r * t).exp() for t in times] + [(-r * t).exp() for t in range(rows)] for r in rates
        ]
        for i in range(NODES):
            best = max(range(i, NODES), key=lambda k: abs(table[k][i]))
            table[i], table[best] = table[best], table[i]
            inverse = 1 / table[i][i]
            table[i] = [v * inverse for v in table[i]]
            for k in range(NODES):
                if k != i:
                    factor = table[k][i]
                    table[k] = [a - factor * b for a, b in zip(table[k], table[i])]
        basis = np.array([[float(v) for v in table[i][NODES:]] for i in range(NODES)], np.float64)
    return [float(t) for t in times], basis


def make_tables(rows):
    times, basis = separable_basis(rows)
    place = np.arange(rows)
    delta = place[:, None] - place[None, :]
    wrapped = basis[:, delta % rows]
    lower = np.where(delta[None] >= 0, wrapped, 0.0)
    upper = np.where(delta[None] < 0, wrapped, 0.0)
    near = np.concatenate(list(lower), axis=1).astype(np.float32)
    far = np.concatenate(list(upper) + [basis.T, np.zeros((rows, 2 * PADDED - NODES))], axis=1).astype(np.float32)
    moments = np.zeros((PADDED, rows), np.float32)
    moments[:NODES] = basis[:, ::-1]
    high = moments.astype(jnp.bfloat16)
    low = (moments - high.astype(np.float32)).astype(jnp.bfloat16)
    last = [float(v) for v in basis[:, rows - 1]]
    return times, last, near.astype(jnp.bfloat16), far.astype(jnp.bfloat16), np.concatenate([high, low], axis=0)


def shifted(whole, offset, rim):
    rolled = pltpu.roll(whole, offset, axis=0)
    top = rolled[:8]
    row = lax.broadcasted_iota(jnp.int32, top.shape, 0)
    for r in range(offset):
        at = None if rim is None else rim.shape[0] - offset + r
        top = jnp.where(row == r, 0.0 if rim is None else rim[at : at + 1], top)
    return top if whole.shape[0] == 8 else jnp.concatenate([top, rolled[8:]], axis=0)


def featurize(signal, taps, rim=None):
    whole = signal.astype(jnp.float32)
    result = taps[0:1] * whole
    for offset in range(1, taps.shape[0]):
        result = result + taps[offset : offset + 1] * shifted(whole, offset, rim)
    return result


def columns(start, stop, step):
    return [(at, min(at + step, stop)) for at in range(start, stop, step)]


def early_kernel(key_ref, value_ref, taps_ref, mixed_ref, key_vmem, value_vmem, taps_vmem, sems):
    rows, width = mixed_ref.shape
    spans = columns(0, width, 256)
    taps_copy = pltpu.make_async_copy(taps_ref.at[:, :, pl.ds(0, width)], taps_vmem, sems.at[0])
    taps_copy.start()
    copies = []
    for n, (a, b) in enumerate(spans):
        at = pl.ds(a, b - a)
        pair = (
            pltpu.make_async_copy(key_ref.at[:, at], key_vmem.at[:, at], sems.at[1 + 2 * n]),
            pltpu.make_async_copy(value_ref.at[:, at], value_vmem.at[:, at], sems.at[2 + 2 * n]),
        )
        for copy in pair:
            copy.start()
        copies.append(pair)
    taps_copy.wait()
    for (a, b), pair in zip(spans, copies):
        for copy in pair:
            copy.wait()
        kf = featurize(key_vmem[:, a:b], taps_vmem[1, :, a:b])
        vf = featurize(value_vmem[:, a:b], taps_vmem[2, :, a:b])
        mixed_ref[:, a:b] = (kf * vf).astype(mixed_ref.dtype)


def second_kernel(
    start, edge, _, query_ref, key_ref, value_ref, taps_ref, residue_ref, rate_ref, mixed_ref, rims_ref, taps_vmem,
    residue_vmem, rate_vmem, key_vmem, value_vmem, held, sems,
):
    rows, width = mixed_ref.shape
    whole = key_ref.shape[1]
    count = 0

    def copy(source, target):
        nonlocal count
        made = pltpu.make_async_copy(source, target, sems.at[count])
        made.start()
        count += 1
        return made

    taps_copy = copy(taps_ref, taps_vmem)
    spans = columns(0, width, 256)
    copies = [
        [
            copy(ref.at[:, pl.ds(start + a, b - a)], vmem.at[:, pl.ds(a, b - a)])
            for ref, vmem in ((key_ref, key_vmem), (value_ref, value_vmem))
        ]
        for a, b in spans
    ]
    rest = [copy(ref.at[pl.ds(rows - 8, 8)], held.at[n]) for n, ref in enumerate((query_ref, key_ref, value_ref))]
    rest += [copy(residue_ref, residue_vmem), copy(rate_ref, rate_vmem)]
    taps_copy.wait()
    for (a, b), pair in zip(spans, copies):
        for made in pair:
            made.wait()
        kf = featurize(key_vmem[:, a:b], taps_vmem[1, :, start + a : start + b])
        vf = featurize(value_vmem[:, a:b], taps_vmem[2, :, start + a : start + b])
        mixed_ref[:, a:b] = (kf * vf).astype(mixed_ref.dtype)
    for made in rest:
        made.wait()
    for n in range(held.shape[0]):
        rims_ref[:, n * whole : (n + 1) * whole] = held[n][8 - edge :]


def pass_kernel(*refs):
    del refs


def prepare_kernel(
    times, rows, key_ref, value_ref, residue_ref, rate_ref, moment_ref, c1, c2, near_ref, far_ref, state_ref, first_ref,
    second_ref, decay_ref, spread_ref, key_vmem, value_vmem, sems,
):
    modes, width = rate_ref.shape
    keep = (lax.axis_index("seq") >= 2).astype(jnp.float32)
    early, late = c1.shape[1], state_ref.shape[1]
    copies = []
    for ref, vmem in ((key_ref, key_vmem), (value_ref, value_vmem)):
        for tall, a, b in ((rows, late, width), (16, 0, late)):
            at = (pl.ds(0, tall), pl.ds(a, b - a))
            copies.append(pltpu.make_async_copy(ref.at[at], vmem.at[at], sems.at[len(copies)]))
            copies[-1].start()
    for c, d in columns(0, early, 256) + columns(early, late, 256) + columns(late, width, 256):
        weights, rates = residue_ref[:, c:d], rate_ref[:, c:d]
        far_weights = weights * jnp.exp(-rates * float(rows))
        later = weights * jnp.exp(-rates)
        near, far = [], []
        for j, t in enumerate(times):
            decay = jnp.exp(-rates * t)
            near.append(jnp.sum(weights * decay, axis=0, keepdims=True))
            far.append(jnp.sum(far_weights * decay, axis=0, keepdims=True))
            decay_ref[j * modes : (j + 1) * modes, c:d] = decay
            spread_ref[j * modes : (j + 1) * modes, c:d] = later * decay
        blank = [jnp.zeros((PADDED - NODES, d - c), jnp.float32)]
        near_ref[:, c:d] = jnp.concatenate(near + blank, axis=0)
        far_ref[:, c:d] = jnp.concatenate(far + blank, axis=0) * keep
        if c < late:
            part = c1[:, c:d] if c < early else c2[:, c - early : d - early]
            state_ref[:, c:d] = modal_state(moment_ref, part, decay_ref, c, d)
            first_ref[:, c:d] = jnp.exp(-rates * float(rows - 1))
            second_ref[:, c:d] = jnp.exp(-rates * float(rows - 2))
    for copy in copies:
        copy.wait()


def modal_state(moment_ref, mixed, decay_ref, c, d):
    halves = jnp.dot(moment_ref[...], mixed, preferred_element_type=jnp.float32)
    moments = halves[:PADDED] + halves[PADDED:]
    modes = decay_ref.shape[0] // NODES
    state = decay_ref[0:modes, c:d] * moments[0:1]
    for j in range(1, NODES):
        state = state + decay_ref[j * modes : (j + 1) * modes, c:d] * moments[j : j + 1]
    return state


def edge_kernel(
    key_ref, value_ref, rims_ref, taps_ref, moment_ref, c1, c2, state_ref, first_ref, second_ref, decay_ref,
    spread_ref, head_ref, middle_ref, *late,
):
    width = key_ref.shape[1]
    early = c1.shape[1] + c2.shape[1]
    modes = state_ref.shape[0]
    keep = (lax.axis_index("seq") >= 1).astype(jnp.float32)
    offset = 0
    for chunk in (c1, c2, *late):
        for a, b in columns(0, chunk.shape[1], 256):
            c, d = offset + a, offset + b
            key_rim = rims_ref[:, width + c : width + d].astype(jnp.float32) * keep
            value_rim = rims_ref[:, 2 * width + c : 2 * width + d].astype(jnp.float32) * keep
            if c < early:
                kf = featurize(key_ref[0:16, c:d].astype(jnp.float32)[:8], taps_ref[1, :, c:d], key_rim)
                vf = featurize(value_ref[0:16, c:d].astype(jnp.float32)[:8], taps_ref[2, :, c:d], value_rim)
                head = (kf * vf).astype(jnp.bfloat16)
                delta = head.astype(jnp.float32) - chunk[0:16, a:b].astype(jnp.float32)[:8]
                state = state_ref[:, c:d] + first_ref[:, c:d] * delta[0:1] + second_ref[:, c:d] * delta[1:2]
            else:
                kf = featurize(key_ref[:, c:d], taps_ref[1, :, c:d], key_rim)
                vf = featurize(value_ref[:, c:d], taps_ref[2, :, c:d], value_rim)
                mixed = (kf * vf).astype(jnp.bfloat16)
                head = mixed[:8]
                state = modal_state(moment_ref, mixed, decay_ref, c, d)
                slot = c - early
                if slot < early:
                    second = head_ref[:, slot : slot + b - a].astype(jnp.float32)[1:2]
                    whole = (kf * vf)[:16]
                    row = lax.broadcasted_iota(jnp.int32, whole.shape, 0)
                    chunk[0:16, a:b] = jnp.where(row == 0, second, whole).astype(jnp.bfloat16)
                    chunk[16:, a:b] = mixed[16:]
                else:
                    chunk[:, a:b] = mixed
            head_ref[:, c:d] = head
            middle = [
                jnp.sum(spread_ref[i * modes : (i + 1) * modes, c:d] * state, axis=0, keepdims=True)
                for i in range(NODES)
            ]
            middle.append(jnp.zeros((PADDED - NODES, d - c), jnp.float32))
            middle_ref[:, c:d] = jnp.concatenate(middle, axis=0).astype(middle_ref.dtype)
        offset = offset + chunk.shape[1]


def own_kernel(edge, start, query_ref, head_ref, near_ref, taps_ref, rims_ref, skip_ref, table_ref, *refs):
    *chunks, part_ref, gate_ref, stack_ref = refs
    rows, _ = query_ref.shape
    keep = (lax.axis_index("seq") >= 1).astype(jnp.float32)
    offset = start
    for chunk in chunks:
        for a, b in columns(0, chunk.shape[1], stack_ref.shape[1]):
            c, d = offset + a, offset + b
            mixed = chunk[:, a:b].astype(jnp.float32)
            mixed = jnp.concatenate([head_ref[:, c:d].astype(jnp.float32), mixed[8:]], axis=0)
            for j in range(NODES):
                stack_ref[j * rows : (j + 1) * rows, : b - a] = (mixed * near_ref[j : j + 1, c:d]).astype(stack_ref.dtype)
            conv = jnp.dot(table_ref[...], stack_ref[:, : b - a], preferred_element_type=jnp.float32)
            part_ref[:, c - start : d - start] = conv + skip_ref[:, c:d] * mixed
            rim = rims_ref[:, c:d].astype(jnp.float32) * keep
            gate_ref[:, c - start : d - start] = featurize(query_ref[:, c:d], taps_ref[0, :, c:d], rim)
        offset = offset + chunk.shape[1]


def finish_kernel(offset, base, slots, last, middle_ref, far_ref, part_ref, gate_ref, table_ref, *refs):
    keep = (lax.axis_index("seq") >= 1).astype(jnp.float32)
    if slots is None:
        _, *backs, out_ref, pre_ref, stack_ref, stage_ref, sems = refs
    else:
        pre_ref, _, *backs, out_ref, stack_ref, stage_ref, repair_ref, sems = refs
    copies = []

    def write(source, rows, c, d):
        copies.append(pltpu.make_async_copy(source, out_ref.at[pl.ds(0, rows), pl.ds(c, d - c)], sems.at[len(copies)]))
        copies[-1].start()

    at = 0
    for back_ref in backs:
        rows, width = back_ref.shape
        for a, b in columns(0, width, stack_ref.shape[1]):
            c, d = offset + at + a, offset + at + b
            back = back_ref[:, a:b].astype(jnp.float32)
            for j in range(NODES):
                stack_ref[j * rows : (j + 1) * rows, : b - a] = (back * far_ref[j : j + 1, c:d]).astype(stack_ref.dtype)
            middle = middle_ref[:, c:d].astype(jnp.float32) * keep
            middle = jnp.concatenate([middle, jnp.zeros_like(middle)], axis=0)
            stack_ref[NODES * rows : NODES * rows + 2 * PADDED, : b - a] = middle.astype(stack_ref.dtype)
            conv = jnp.dot(table_ref[...], stack_ref[:, : b - a], preferred_element_type=jnp.float32)
            total = part_ref[:, c - base : d - base] + conv
            gate = gate_ref[:, c - base : d - base]
            stage_ref[:, at + a : at + b] = (gate * total).astype(stage_ref.dtype)
            write(stage_ref.at[:, pl.ds(at + a, b - a)], rows, c, d)
            if slots is None:
                pre_ref[0:16, c:d] = total[:16]
                pre_ref[16:32, c:d] = gate[:16]
                pre_ref[32:40, c:d] = back[:8]
        at = at + width
    start = 0
    for (first, stop), back_ref in zip(slots or (), backs):
        for c, d in columns(first, stop, 512):
            end = far_ref[0:1, c:d] * last[0]
            for j in range(1, NODES):
                end = end + far_ref[j : j + 1, c:d] * last[j]
            right = back_ref[0:16, c - first : d - first].astype(jnp.float32)[0:1]
            total = pre_ref[0:16, c:d]
            row = lax.broadcasted_iota(jnp.int32, total.shape, 0)
            total = jnp.where(row == 0, total + end * (right - pre_ref[33:34, c:d]), total)
            repair_ref[:, start + c - first : start + d - first] = (pre_ref[16:32, c:d] * total).astype(repair_ref.dtype)
        if stop > first:
            write(repair_ref.at[:, pl.ds(start, stop - first)], 16, first, stop)
        start = start + stop - first
    for copy in copies:
        copy.wait()


def ring(array, by, closed=True):
    length = lax.axis_size("seq")
    return lax.ppermute(
        array, "seq", [(i, (i + by) % length) for i in range(length) if closed or i + by < length]
    )


def shards(query_in, key_in, value_in, short_filter, residue, rate, skip):
    rows, width = query_in.shape
    kinds, count, _ = short_filter.shape
    edge = count - 1
    modes = residue.shape[1]
    times, last, near_table, far_table, moment_table = make_tables(rows)
    near_table, far_table, moment_table = (jnp.asarray(t) for t in (near_table, far_table, moment_table))
    residue_t, rate_t, skip_row = residue.T, rate.T, skip.reshape(1, width)
    unit = width // 32
    cuts = [0, 7 * unit, 15 * unit, 21 * unit, 27 * unit, 32 * unit]
    count_chunks = len(cuts) - 1
    sizes = [cuts[i + 1] - cuts[i] for i in range(count_chunks)]
    bf16, f32 = jnp.bfloat16, jnp.float32
    vmem, hbm, anywhere = (pl.BlockSpec(memory_space=m) for m in (pltpu.VMEM, pltpu.HBM, pl.ANY))

    def call(body, ins, outs, operands, scratch=(), limit=40, cost=1, **kw):
        return pl.pallas_call(
            body,
            in_specs=ins,
            out_specs=[o[2] if len(o) > 2 else vmem for o in outs],
            out_shape=[jax.ShapeDtypeStruct(o[0], o[1]) for o in outs],
            scratch_shapes=list(scratch),
            compiler_params=pltpu.CompilerParams(vmem_limit_bytes=limit * 1024 * 1024),
            cost_estimate=pl.CostEstimate(flops=cost, bytes_accessed=cost, transcendentals=0),
            **kw,
        )(*(pltpu.with_memory_space_constraint(x, pltpu.HBM) if i is hbm else x for i, x in zip(ins, operands)))

    back = [None] * count_chunks
    (c1,) = call(
        early_kernel,
        [hbm] * 3,
        [((rows, sizes[0]), bf16)],
        (key_in, value_in, short_filter),
        [
            pltpu.VMEM((rows, sizes[0]), bf16),
            pltpu.VMEM((rows, sizes[0]), bf16),
            pltpu.VMEM((kinds, count, sizes[0]), f32),
            pltpu.SemaphoreType.DMA((1 + 2 * len(columns(0, sizes[0], 256)),)),
        ],
    )
    back[0] = ring(c1, 2)
    c2, rims, taps_v, residue_v, rate_v = call(
        functools.partial(second_kernel, cuts[1], edge),
        [anywhere] + [hbm] * 6,
        [
            ((rows, sizes[1]), bf16),
            ((edge, kinds * width), bf16),
            (short_filter.shape, f32),
            ((modes, width), f32),
            ((modes, width), f32),
        ],
        (c1, query_in, key_in, value_in, short_filter, residue_t, rate_t),
        [
            pltpu.VMEM((rows, sizes[1]), bf16),
            pltpu.VMEM((rows, sizes[1]), bf16),
            pltpu.VMEM((kinds, 8, width), bf16),
            pltpu.SemaphoreType.DMA((3 + kinds + 2 * len(columns(0, sizes[1], 256)),)),
        ],
    )
    rims_in = ring(rims, 1)
    back[1] = ring(c2, 2)
    near, far, *states, key_v, value_v = call(
        functools.partial(prepare_kernel, times, rows),
        [hbm] * 2 + [vmem] * 5,
        [((PADDED, width), f32)] * 2
        + [((modes, cuts[2]), f32)] * 3
        + [((NODES * modes, width), f32)] * 2
        + [((rows, width), bf16)] * 2,
        (key_in, value_in, residue_v, rate_v, moment_table, c1, c2),
        [pltpu.SemaphoreType.DMA((4,))],
    )
    late = range(2, count_chunks)
    head, middle, *chunks = call(
        edge_kernel,
        [vmem] * 12,
        [((8, width), bf16), ((PADDED, width), bf16)] + [((rows, sizes[i]), bf16) for i in late],
        (key_v, value_v, rims_in, taps_v, moment_table, c1, c2, *states),
    )
    middle_in = ring(middle, 1)
    for i in late[:-1]:
        back[i] = ring(chunks[i - 2], 2, closed=i < late[-2])

    tile = 512

    def own(first, stop, some):
        return call(
            functools.partial(own_kernel, edge, cuts[first]),
            [vmem] * (7 + len(some)),
            [((rows, cuts[stop] - cuts[first]), f32)] * 2,
            (query_in, head, near, taps_v, rims_in, skip_row, near_table, *some),
            [pltpu.VMEM((near_table.shape[1], tile), bf16)],
        )

    early_own = own(0, 2, (c1, c2))
    (final,) = call(
        pass_kernel,
        [anywhere] * 4,
        [((rows, sizes[-1]), bf16, anywhere)],
        (middle_in, early_own[0], back[0], chunks[-1]),
        input_output_aliases={3: 0},
    )
    back[-1] = ring(final, 2, closed=False)
    late_own = own(2, count_chunks, chunks)

    def finish(first, stop, out, pre):
        some = range(first, stop)
        size = cuts[stop] - cuts[first]
        step = tile if stop < count_chunks else LAST_TILE
        pieces = sum(len(columns(0, sizes[i], step)) for i in some)
        scratch = [pltpu.VMEM((far_table.shape[1], step), bf16), pltpu.VMEM((rows, size), bf16)]
        slots = None
        if out is not None:
            slots = [(min(cuts[i] - cuts[2], cuts[2]), min(cuts[i + 1] - cuts[2], cuts[2])) for i in some]
            scratch.append(pltpu.VMEM((16, max(sum(b - a for a, b in slots), unit)), bf16))
        scratch.append(pltpu.SemaphoreType.DMA((pieces + len(some),)))
        return call(
            functools.partial(finish_kernel, cuts[first], cuts[0 if out is None else 2], slots, last),
            [vmem] * 5 + ([anywhere] if out is None else [vmem, anywhere]) + [vmem] * len(some),
            [((rows, width), bf16, anywhere)] + ([((40, cuts[2]), f32)] if out is None else []),
            (middle_in, far, *(early_own if out is None else late_own), far_table)
            + ((late_own[0],) if out is None else (pre, out))
            + tuple(back[i] for i in some),
            scratch,
            input_output_aliases={} if out is None else {6: 0},
        )

    out, pre = finish(0, 2, None, None)
    (out,) = finish(2, count_chunks - 1, out, pre)
    (out,) = finish(count_chunks - 1, count_chunks, out, pre)
    return out


def solution(mesh):
    return jax.shard_map(
        shards,
        mesh=mesh,
        in_specs=(P(("grp", "seq"), None),) * 3 + (P(),) * 4,
        out_specs=P(("grp", "seq"), None),
        check_vma=False,
    )
```

```python
import functools
import math
from decimal import Decimal, localcontext

import jax
import jax.numpy as jnp
import numpy as np
from jax import lax
from jax.experimental import pallas as pl
from jax.experimental.pallas import tpu as pltpu
from jax.sharding import PartitionSpec as P

RATE_LOW, RATE_HIGH = 0.000390625, 0.03
NODES = 7
PADDED = 8
LAST_TILE = 256


def separable_basis(rows):
    cosines = [math.cos(math.pi * (j + 0.5) / NODES) for j in range(NODES)]
    with localcontext() as context:
        context.prec = 50
        times = [Decimal(str(round((rows - 1) / 2 * (1 - v), 2))) for v in cosines]
        span = RATE_HIGH - RATE_LOW
        rates = [Decimal(str(round(RATE_LOW + span * ((1 - v) / 2) ** 1.3, 6))) for v in cosines]
        table = [
            [(-r * t).exp() for t in times] + [(-r * t).exp() for t in range(rows)] for r in rates
        ]
        for i in range(NODES):
            best = max(range(i, NODES), key=lambda k: abs(table[k][i]))
            table[i], table[best] = table[best], table[i]
            inverse = 1 / table[i][i]
            table[i] = [v * inverse for v in table[i]]
            for k in range(NODES):
                if k != i:
                    factor = table[k][i]
                    table[k] = [a - factor * b for a, b in zip(table[k], table[i])]
        basis = np.array([[float(v) for v in table[i][NODES:]] for i in range(NODES)], np.float64)
    return [float(t) for t in times], basis


def make_tables(rows):
    times, basis = separable_basis(rows)
    place = np.arange(rows)
    delta = place[:, None] - place[None, :]
    wrapped = basis[:, delta % rows]
    lower = np.where(delta[None] >= 0, wrapped, 0.0)
    upper = np.where(delta[None] < 0, wrapped, 0.0)
    near = np.concatenate(list(lower), axis=1).astype(np.float32)
    far = np.concatenate(list(upper) + [basis.T, np.zeros((rows, 2 * PADDED - NODES))], axis=1).astype(np.float32)
    moments = np.zeros((PADDED, rows), np.float32)
    moments[:NODES] = basis[:, ::-1]
    high = moments.astype(jnp.bfloat16)
    low = (moments - high.astype(np.float32)).astype(jnp.bfloat16)
    last = [float(v) for v in basis[:, rows - 1]]
    return times, last, near.astype(jnp.bfloat16), far.astype(jnp.bfloat16), np.concatenate([high, low], axis=0)


def shifted(whole, offset, rim):
    rolled = pltpu.roll(whole, offset, axis=0)
    top = rolled[:8]
    row = lax.broadcasted_iota(jnp.int32, top.shape, 0)
    for r in range(offset):
        at = None if rim is None else rim.shape[0] - offset + r
        top = jnp.where(row == r, 0.0 if rim is None else rim[at : at + 1], top)
    return top if whole.shape[0] == 8 else jnp.concatenate([top, rolled[8:]], axis=0)


def featurize(signal, taps, rim=None):
    whole = signal.astype(jnp.float32)
    result = taps[0:1] * whole
    for offset in range(1, taps.shape[0]):
        result = result + taps[offset : offset + 1] * shifted(whole, offset, rim)
    return result


def columns(start, stop, step):
    return [(at, min(at + step, stop)) for at in range(start, stop, step)]


def early_kernel(key_ref, value_ref, taps_ref, mixed_ref, key_vmem, value_vmem, taps_vmem, sems):
    rows, width = mixed_ref.shape
    spans = columns(0, width, 256)
    taps_copy = pltpu.make_async_copy(taps_ref.at[:, :, pl.ds(0, width)], taps_vmem, sems.at[0])
    taps_copy.start()
    copies = []
    for n, (a, b) in enumerate(spans):
        at = pl.ds(a, b - a)
        pair = (
            pltpu.make_async_copy(key_ref.at[:, at], key_vmem.at[:, at], sems.at[1 + 2 * n]),
            pltpu.make_async_copy(value_ref.at[:, at], value_vmem.at[:, at], sems.at[2 + 2 * n]),
        )
        for copy in pair:
            copy.start()
        copies.append(pair)
    taps_copy.wait()
    for (a, b), pair in zip(spans, copies):
        for copy in pair:
            copy.wait()
        kf = featurize(key_vmem[:, a:b], taps_vmem[1, :, a:b])
        vf = featurize(value_vmem[:, a:b], taps_vmem[2, :, a:b])
        mixed_ref[:, a:b] = (kf * vf).astype(mixed_ref.dtype)


def second_kernel(
    start, edge, _, query_ref, key_ref, value_ref, taps_ref, residue_ref, rate_ref, mixed_ref, rims_ref, taps_vmem,
    residue_vmem, rate_vmem, key_vmem, value_vmem, held, sems,
):
    rows, width = mixed_ref.shape
    whole = key_ref.shape[1]
    count = 0

    def copy(source, target):
        nonlocal count
        made = pltpu.make_async_copy(source, target, sems.at[count])
        made.start()
        count += 1
        return made

    taps_copy = copy(taps_ref, taps_vmem)
    spans = columns(0, width, 256)
    copies = [
        [
            copy(ref.at[:, pl.ds(start + a, b - a)], vmem.at[:, pl.ds(a, b - a)])
            for ref, vmem in ((key_ref, key_vmem), (value_ref, value_vmem))
        ]
        for a, b in spans
    ]
    rest = [copy(ref.at[pl.ds(rows - 8, 8)], held.at[n]) for n, ref in enumerate((query_ref, key_ref, value_ref))]
    rest += [copy(residue_ref, residue_vmem), copy(rate_ref, rate_vmem)]
    taps_copy.wait()
    for (a, b), pair in zip(spans, copies):
        for made in pair:
            made.wait()
        kf = featurize(key_vmem[:, a:b], taps_vmem[1, :, start + a : start + b])
        vf = featurize(value_vmem[:, a:b], taps_vmem[2, :, start + a : start + b])
        mixed_ref[:, a:b] = (kf * vf).astype(mixed_ref.dtype)
    for made in rest:
        made.wait()
    for n in range(held.shape[0]):
        rims_ref[:, n * whole : (n + 1) * whole] = held[n][8 - edge :]


def pass_kernel(*refs):
    del refs


def prepare_kernel(
    times, rows, key_ref, value_ref, residue_ref, rate_ref, moment_ref, c1, c2, near_ref, far_ref, state_ref, first_ref,
    second_ref, decay_ref, spread_ref, key_vmem, value_vmem, sems,
):
    modes, width = rate_ref.shape
    keep = (lax.axis_index("seq") >= 2).astype(jnp.float32)
    early, late = c1.shape[1], state_ref.shape[1]
    copies = []
    for ref, vmem in ((key_ref, key_vmem), (value_ref, value_vmem)):
        for tall, a, b in ((rows, late, width), (16, 0, late)):
            at = (pl.ds(0, tall), pl.ds(a, b - a))
            copies.append(pltpu.make_async_copy(ref.at[at], vmem.at[at], sems.at[len(copies)]))
            copies[-1].start()
    for c, d in columns(0, early, 256) + columns(early, late, 256) + columns(late, width, 256):
        weights, rates = residue_ref[:, c:d], rate_ref[:, c:d]
        far_weights = weights * jnp.exp(-rates * float(rows))
        later = weights * jnp.exp(-rates)
        near, far = [], []
        for j, t in enumerate(times):
            decay = jnp.exp(-rates * t)
            near.append(jnp.sum(weights * decay, axis=0, keepdims=True))
            far.append(jnp.sum(far_weights * decay, axis=0, keepdims=True))
            decay_ref[j * modes : (j + 1) * modes, c:d] = decay
            spread_ref[j * modes : (j + 1) * modes, c:d] = later * decay
        blank = [jnp.zeros((PADDED - NODES, d - c), jnp.float32)]
        near_ref[:, c:d] = jnp.concatenate(near + blank, axis=0)
        far_ref[:, c:d] = jnp.concatenate(far + blank, axis=0) * keep
        if c < late:
            part = c1[:, c:d] if c < early else c2[:, c - early : d - early]
            state_ref[:, c:d] = modal_state(moment_ref, part, decay_ref, c, d)
            first_ref[:, c:d] = jnp.exp(-rates * float(rows - 1))
            second_ref[:, c:d] = jnp.exp(-rates * float(rows - 2))
    for copy in copies:
        copy.wait()


def modal_state(moment_ref, mixed, decay_ref, c, d):
    halves = jnp.dot(moment_ref[...], mixed, preferred_element_type=jnp.float32)
    moments = halves[:PADDED] + halves[PADDED:]
    modes = decay_ref.shape[0] // NODES
    state = decay_ref[0:modes, c:d] * moments[0:1]
    for j in range(1, NODES):
        state = state + decay_ref[j * modes : (j + 1) * modes, c:d] * moments[j : j + 1]
    return state


def edge_kernel(
    key_ref, value_ref, rims_ref, taps_ref, moment_ref, c1, c2, state_ref, first_ref, second_ref, decay_ref,
    spread_ref, head_ref, middle_ref, *late,
):
    width = key_ref.shape[1]
    early = c1.shape[1] + c2.shape[1]
    modes = state_ref.shape[0]
    keep = (lax.axis_index("seq") >= 1).astype(jnp.float32)
    offset = 0
    for chunk in (c1, c2, *late):
        for a, b in columns(0, chunk.shape[1], 256):
            c, d = offset + a, offset + b
            key_rim = rims_ref[:, width + c : width + d].astype(jnp.float32) * keep
            value_rim = rims_ref[:, 2 * width + c : 2 * width + d].astype(jnp.float32) * keep
            if c < early:
                kf = featurize(key_ref[0:16, c:d].astype(jnp.float32)[:8], taps_ref[1, :, c:d], key_rim)
                vf = featurize(value_ref[0:16, c:d].astype(jnp.float32)[:8], taps_ref[2, :, c:d], value_rim)
                head = (kf * vf).astype(jnp.bfloat16)
                delta = head.astype(jnp.float32) - chunk[0:16, a:b].astype(jnp.float32)[:8]
                state = state_ref[:, c:d] + first_ref[:, c:d] * delta[0:1] + second_ref[:, c:d] * delta[1:2]
            else:
                kf = featurize(key_ref[:, c:d], taps_ref[1, :, c:d], key_rim)
                vf = featurize(value_ref[:, c:d], taps_ref[2, :, c:d], value_rim)
                mixed = (kf * vf).astype(jnp.bfloat16)
                head = mixed[:8]
                state = modal_state(moment_ref, mixed, decay_ref, c, d)
                slot = c - early
                if slot < early:
                    second = head_ref[:, slot : slot + b - a].astype(jnp.float32)[1:2]
                    whole = (kf * vf)[:16]
                    row = lax.broadcasted_iota(jnp.int32, whole.shape, 0)
                    chunk[0:16, a:b] = jnp.where(row == 0, second, whole).astype(jnp.bfloat16)
                    chunk[16:, a:b] = mixed[16:]
                else:
                    chunk[:, a:b] = mixed
            head_ref[:, c:d] = head
            middle = [
                jnp.sum(spread_ref[i * modes : (i + 1) * modes, c:d] * state, axis=0, keepdims=True)
                for i in range(NODES)
            ]
            middle.append(jnp.zeros((PADDED - NODES, d - c), jnp.float32))
            middle_ref[:, c:d] = jnp.concatenate(middle, axis=0).astype(middle_ref.dtype)
        offset = offset + chunk.shape[1]


def own_kernel(edge, start, query_ref, head_ref, near_ref, taps_ref, rims_ref, skip_ref, table_ref, *refs):
    *chunks, part_ref, gate_ref, stack_ref = refs
    rows, _ = query_ref.shape
    keep = (lax.axis_index("seq") >= 1).astype(jnp.float32)
    offset = start
    for chunk in chunks:
        for a, b in columns(0, chunk.shape[1], stack_ref.shape[1]):
            c, d = offset + a, offset + b
            mixed = chunk[:, a:b].astype(jnp.float32)
            mixed = jnp.concatenate([head_ref[:, c:d].astype(jnp.float32), mixed[8:]], axis=0)
            for j in range(NODES):
                stack_ref[j * rows : (j + 1) * rows, : b - a] = (mixed * near_ref[j : j + 1, c:d]).astype(stack_ref.dtype)
            conv = jnp.dot(table_ref[...], stack_ref[:, : b - a], preferred_element_type=jnp.float32)
            part_ref[:, c - start : d - start] = conv + skip_ref[:, c:d] * mixed
            rim = rims_ref[:, c:d].astype(jnp.float32) * keep
            gate_ref[:, c - start : d - start] = featurize(query_ref[:, c:d], taps_ref[0, :, c:d], rim)
        offset = offset + chunk.shape[1]


def finish_kernel(offset, base, slots, last, middle_ref, far_ref, part_ref, gate_ref, table_ref, *refs):
    keep = (lax.axis_index("seq") >= 1).astype(jnp.float32)
    if slots is None:
        _, *backs, out_ref, pre_ref, stack_ref, stage_ref, sems = refs
    else:
        pre_ref, _, *backs, out_ref, stack_ref, stage_ref, repair_ref, sems = refs
    copies = []

    def write(source, rows, c, d):
        copies.append(pltpu.make_async_copy(source, out_ref.at[pl.ds(0, rows), pl.ds(c, d - c)], sems.at[len(copies)]))
        copies[-1].start()

    at = 0
    for back_ref in backs:
        rows, width = back_ref.shape
        for a, b in columns(0, width, stack_ref.shape[1]):
            c, d = offset + at + a, offset + at + b
            back = back_ref[:, a:b].astype(jnp.float32)
            for j in range(NODES):
                stack_ref[j * rows : (j + 1) * rows, : b - a] = (back * far_ref[j : j + 1, c:d]).astype(stack_ref.dtype)
            middle = middle_ref[:, c:d].astype(jnp.float32) * keep
            middle = jnp.concatenate([middle, jnp.zeros_like(middle)], axis=0)
            stack_ref[NODES * rows : NODES * rows + 2 * PADDED, : b - a] = middle.astype(stack_ref.dtype)
            conv = jnp.dot(table_ref[...], stack_ref[:, : b - a], preferred_element_type=jnp.float32)
            total = part_ref[:, c - base : d - base] + conv
            gate = gate_ref[:, c - base : d - base]
            stage_ref[:, at + a : at + b] = (gate * total).astype(stage_ref.dtype)
            write(stage_ref.at[:, pl.ds(at + a, b - a)], rows, c, d)
            if slots is None:
                pre_ref[0:16, c:d] = total[:16]
                pre_ref[16:32, c:d] = gate[:16]
                pre_ref[32:40, c:d] = back[:8]
        at = at + width
    start = 0
    for (first, stop), back_ref in zip(slots or (), backs):
        for c, d in columns(first, stop, 512):
            end = far_ref[0:1, c:d] * last[0]
            for j in range(1, NODES):
                end = end + far_ref[j : j + 1, c:d] * last[j]
            right = back_ref[0:16, c - first : d - first].astype(jnp.float32)[0:1]
            total = pre_ref[0:16, c:d]
            row = lax.broadcasted_iota(jnp.int32, total.shape, 0)
            total = jnp.where(row == 0, total + end * (right - pre_ref[33:34, c:d]), total)
            repair_ref[:, start + c - first : start + d - first] = (pre_ref[16:32, c:d] * total).astype(repair_ref.dtype)
        if stop > first:
            write(repair_ref.at[:, pl.ds(start, stop - first)], 16, first, stop)
        start = start + stop - first
    for copy in copies:
        copy.wait()


def ring(array, by, closed=True):
    length = lax.axis_size("seq")
    return lax.ppermute(
        array, "seq", [(i, (i + by) % length) for i in range(length) if closed or i + by < length]
    )


def shards(query_in, key_in, value_in, short_filter, residue, rate, skip):
    rows, width = query_in.shape
    kinds, count, _ = short_filter.shape
    edge = count - 1
    modes = residue.shape[1]
    times, last, near_table, far_table, moment_table = make_tables(rows)
    near_table, far_table, moment_table = (jnp.asarray(t) for t in (near_table, far_table, moment_table))
    residue_t, rate_t, skip_row = residue.T, rate.T, skip.reshape(1, width)
    unit = width // 32
    cuts = [0, 7 * unit, 15 * unit, 21 * unit, 27 * unit, 32 * unit]
    count_chunks = len(cuts) - 1
    sizes = [cuts[i + 1] - cuts[i] for i in range(count_chunks)]
    bf16, f32 = jnp.bfloat16, jnp.float32
    vmem, hbm, anywhere = (pl.BlockSpec(memory_space=m) for m in (pltpu.VMEM, pltpu.HBM, pl.ANY))

    def call(body, ins, outs, operands, scratch=(), limit=40, cost=1, **kw):
        return pl.pallas_call(
            body,
            in_specs=ins,
            out_specs=[o[2] if len(o) > 2 else vmem for o in outs],
            out_shape=[jax.ShapeDtypeStruct(o[0], o[1]) for o in outs],
            scratch_shapes=list(scratch),
            compiler_params=pltpu.CompilerParams(vmem_limit_bytes=limit * 1024 * 1024),
            cost_estimate=pl.CostEstimate(flops=cost, bytes_accessed=cost, transcendentals=0),
            **kw,
        )(*(pltpu.with_memory_space_constraint(x, pltpu.HBM) if i is hbm else x for i, x in zip(ins, operands)))

    back = [None] * count_chunks
    (c1,) = call(
        early_kernel,
        [hbm] * 3,
        [((rows, sizes[0]), bf16)],
        (key_in, value_in, short_filter),
        [
            pltpu.VMEM((rows, sizes[0]), bf16),
            pltpu.VMEM((rows, sizes[0]), bf16),
            pltpu.VMEM((kinds, count, sizes[0]), f32),
            pltpu.SemaphoreType.DMA((1 + 2 * len(columns(0, sizes[0], 256)),)),
        ],
    )
    back[0] = ring(c1, 2)
    c2, rims, taps_v, residue_v, rate_v = call(
        functools.partial(second_kernel, cuts[1], edge),
        [anywhere] + [hbm] * 6,
        [
            ((rows, sizes[1]), bf16),
            ((edge, kinds * width), bf16),
            (short_filter.shape, f32),
            ((modes, width), f32),
            ((modes, width), f32),
        ],
        (c1, query_in, key_in, value_in, short_filter, residue_t, rate_t),
        [
            pltpu.VMEM((rows, sizes[1]), bf16),
            pltpu.VMEM((rows, sizes[1]), bf16),
            pltpu.VMEM((kinds, 8, width), bf16),
            pltpu.SemaphoreType.DMA((3 + kinds + 2 * len(columns(0, sizes[1], 256)),)),
        ],
    )
    rims_in = ring(rims, 1)
    back[1] = ring(c2, 2)
    near, far, *states, key_v, value_v = call(
        functools.partial(prepare_kernel, times, rows),
        [hbm] * 2 + [vmem] * 5,
        [((PADDED, width), f32)] * 2
        + [((modes, cuts[2]), f32)] * 3
        + [((NODES * modes, width), f32)] * 2
        + [((rows, width), bf16)] * 2,
        (key_in, value_in, residue_v, rate_v, moment_table, c1, c2),
        [pltpu.SemaphoreType.DMA((4,))],
    )
    late = range(2, count_chunks)
    head, middle, *chunks = call(
        edge_kernel,
        [vmem] * 12,
        [((8, width), bf16), ((PADDED, width), bf16)] + [((rows, sizes[i]), bf16) for i in late],
        (key_v, value_v, rims_in, taps_v, moment_table, c1, c2, *states),
    )
    middle_in = ring(middle, 1)
    for i in late[:-1]:
        back[i] = ring(chunks[i - 2], 2, closed=i < late[-2])

    tile = 512

    def own(first, stop, some):
        return call(
            functools.partial(own_kernel, edge, cuts[first]),
            [vmem] * (7 + len(some)),
            [((rows, cuts[stop] - cuts[first]), f32)] * 2,
            (query_in, head, near, taps_v, rims_in, skip_row, near_table, *some),
            [pltpu.VMEM((near_table.shape[1], tile), bf16)],
        )

    early_own = own(0, 2, (c1, c2))
    (final,) = call(
        pass_kernel,
        [anywhere] * 4,
        [((rows, sizes[-1]), bf16, anywhere)],
        (middle_in, early_own[0], back[0], chunks[-1]),
        input_output_aliases={3: 0},
    )
    back[-1] = ring(final, 2, closed=False)
    late_own = own(2, count_chunks, [*chunks[:-1], final])

    def finish(first, stop, out, pre):
        some = range(first, stop)
        size = cuts[stop] - cuts[first]
        step = tile if stop < count_chunks else LAST_TILE
        pieces = sum(len(columns(0, sizes[i], step)) for i in some)
        scratch = [pltpu.VMEM((far_table.shape[1], step), bf16), pltpu.VMEM((rows, size), bf16)]
        slots = None
        if out is not None:
            slots = [(min(cuts[i] - cuts[2], cuts[2]), min(cuts[i + 1] - cuts[2], cuts[2])) for i in some]
            scratch.append(pltpu.VMEM((16, max(sum(b - a for a, b in slots), unit)), bf16))
        scratch.append(pltpu.SemaphoreType.DMA((pieces + len(some),)))
        return call(
            functools.partial(finish_kernel, cuts[first], cuts[0 if out is None else 2], slots, last),
            [vmem] * 5 + ([anywhere] if out is None else [vmem, anywhere]) + [vmem] * len(some),
            [((rows, width), bf16, anywhere)] + ([((40, cuts[2]), f32)] if out is None else []),
            (middle_in, far, *(early_own if out is None else late_own), far_table)
            + ((late_own[0],) if out is None else (pre, out))
            + tuple(back[i] for i in some),
            scratch,
            input_output_aliases={} if out is None else {6: 0},
        )

    out, pre = finish(0, 2, None, None)
    (out,) = finish(2, count_chunks - 1, out, pre)
    (out,) = finish(count_chunks - 1, count_chunks, out, pre)
    return out


def solution(mesh):
    return jax.shard_map(
        shards,
        mesh=mesh,
        in_specs=(P(("grp", "seq"), None),) * 3 + (P(),) * 4,
        out_specs=P(("grp", "seq"), None),
        check_vma=False,
    )
```

```python
import functools
import math
from decimal import Decimal, localcontext

import jax
import jax.numpy as jnp
import numpy as np
from jax import lax
from jax.experimental import pallas as pl
from jax.experimental.pallas import tpu as pltpu
from jax.sharding import PartitionSpec as P

RATE_LOW, RATE_HIGH = 0.000390625, 0.03
NODES = 7
PADDED = 8
LAST_TILE = 256


def separable_basis(rows):
    cosines = [math.cos(math.pi * (j + 0.5) / NODES) for j in range(NODES)]
    with localcontext() as context:
        context.prec = 50
        times = [Decimal(str(round((rows - 1) / 2 * (1 - v), 2))) for v in cosines]
        span = RATE_HIGH - RATE_LOW
        rates = [Decimal(str(round(RATE_LOW + span * ((1 - v) / 2) ** 1.3, 6))) for v in cosines]
        table = [
            [(-r * t).exp() for t in times] + [(-r * t).exp() for t in range(rows)] for r in rates
        ]
        for i in range(NODES):
            best = max(range(i, NODES), key=lambda k: abs(table[k][i]))
            table[i], table[best] = table[best], table[i]
            inverse = 1 / table[i][i]
            table[i] = [v * inverse for v in table[i]]
            for k in range(NODES):
                if k != i:
                    factor = table[k][i]
                    table[k] = [a - factor * b for a, b in zip(table[k], table[i])]
        basis = np.array([[float(v) for v in table[i][NODES:]] for i in range(NODES)], np.float64)
    return [float(t) for t in times], basis


def make_tables(rows):
    times, basis = separable_basis(rows)
    place = np.arange(rows)
    delta = place[:, None] - place[None, :]
    wrapped = basis[:, delta % rows]
    lower = np.where(delta[None] >= 0, wrapped, 0.0)
    upper = np.where(delta[None] < 0, wrapped, 0.0)
    near = np.concatenate(list(lower), axis=1).astype(np.float32)
    far = np.concatenate(list(upper) + [basis.T, np.zeros((rows, 2 * PADDED - NODES))], axis=1).astype(np.float32)
    moments = np.zeros((PADDED, rows), np.float32)
    moments[:NODES] = basis[:, ::-1]
    high = moments.astype(jnp.bfloat16)
    low = (moments - high.astype(np.float32)).astype(jnp.bfloat16)
    last = [float(v) for v in basis[:, rows - 1]]
    return times, last, near.astype(jnp.bfloat16), far.astype(jnp.bfloat16), np.concatenate([high, low], axis=0)


def shifted(whole, offset, rim):
    rolled = pltpu.roll(whole, offset, axis=0)
    top = rolled[:8]
    row = lax.broadcasted_iota(jnp.int32, top.shape, 0)
    for r in range(offset):
        at = None if rim is None else rim.shape[0] - offset + r
        top = jnp.where(row == r, 0.0 if rim is None else rim[at : at + 1], top)
    return top if whole.shape[0] == 8 else jnp.concatenate([top, rolled[8:]], axis=0)


def featurize(signal, taps, rim=None):
    whole = signal.astype(jnp.float32)
    result = taps[0:1] * whole
    for offset in range(1, taps.shape[0]):
        result = result + taps[offset : offset + 1] * shifted(whole, offset, rim)
    return result


def columns(start, stop, step):
    return [(at, min(at + step, stop)) for at in range(start, stop, step)]


def early_kernel(key_ref, value_ref, taps_ref, mixed_ref, key_vmem, value_vmem, taps_vmem, sems):
    rows, width = mixed_ref.shape
    spans = columns(0, width, 256)
    taps_copy = pltpu.make_async_copy(taps_ref.at[:, :, pl.ds(0, width)], taps_vmem, sems.at[0])
    taps_copy.start()
    copies = []
    for n, (a, b) in enumerate(spans):
        at = pl.ds(a, b - a)
        pair = (
            pltpu.make_async_copy(key_ref.at[:, at], key_vmem.at[:, at], sems.at[1 + 2 * n]),
            pltpu.make_async_copy(value_ref.at[:, at], value_vmem.at[:, at], sems.at[2 + 2 * n]),
        )
        for copy in pair:
            copy.start()
        copies.append(pair)
    taps_copy.wait()
    for (a, b), pair in zip(spans, copies):
        for copy in pair:
            copy.wait()
        kf = featurize(key_vmem[:, a:b], taps_vmem[1, :, a:b])
        vf = featurize(value_vmem[:, a:b], taps_vmem[2, :, a:b])
        mixed_ref[:, a:b] = (kf * vf).astype(mixed_ref.dtype)


def second_kernel(
    start, edge, _, query_ref, key_ref, value_ref, taps_ref, residue_ref, rate_ref, mixed_ref, rims_ref, taps_vmem,
    residue_vmem, rate_vmem, key_vmem, value_vmem, held, sems,
):
    rows, width = mixed_ref.shape
    whole = key_ref.shape[1]
    count = 0

    def copy(source, target):
        nonlocal count
        made = pltpu.make_async_copy(source, target, sems.at[count])
        made.start()
        count += 1
        return made

    taps_copy = copy(taps_ref, taps_vmem)
    spans = columns(0, width, 256)
    copies = [
        [
            copy(ref.at[:, pl.ds(start + a, b - a)], vmem.at[:, pl.ds(a, b - a)])
            for ref, vmem in ((key_ref, key_vmem), (value_ref, value_vmem))
        ]
        for a, b in spans
    ]
    rest = [copy(ref.at[pl.ds(rows - 8, 8)], held.at[n]) for n, ref in enumerate((query_ref, key_ref, value_ref))]
    rest += [copy(residue_ref, residue_vmem), copy(rate_ref, rate_vmem)]
    taps_copy.wait()
    for (a, b), pair in zip(spans, copies):
        for made in pair:
            made.wait()
        kf = featurize(key_vmem[:, a:b], taps_vmem[1, :, start + a : start + b])
        vf = featurize(value_vmem[:, a:b], taps_vmem[2, :, start + a : start + b])
        mixed_ref[:, a:b] = (kf * vf).astype(mixed_ref.dtype)
    for made in rest:
        made.wait()
    for n in range(held.shape[0]):
        rims_ref[:, n * whole : (n + 1) * whole] = held[n][8 - edge :]


def prepare_kernel(
    times, rows, key_ref, value_ref, residue_ref, rate_ref, moment_ref, c1, c2, near_ref, far_ref, state_ref, first_ref,
    second_ref, decay_ref, spread_ref, key_vmem, value_vmem, sems,
):
    modes, width = rate_ref.shape
    early, late = c1.shape[1], state_ref.shape[1]
    copies = []
    for ref, vmem in ((key_ref, key_vmem), (value_ref, value_vmem)):
        for tall, a, b in ((rows, late, width), (16, 0, late)):
            at = (pl.ds(0, tall), pl.ds(a, b - a))
            copies.append(pltpu.make_async_copy(ref.at[at], vmem.at[at], sems.at[len(copies)]))
            copies[-1].start()
    for c, d in columns(0, early, 256) + columns(early, late, 256) + columns(late, width, 256):
        weights, rates = residue_ref[:, c:d], rate_ref[:, c:d]
        far_weights = weights * jnp.exp(-rates * float(rows))
        later = weights * jnp.exp(-rates)
        near, far = [], []
        for j, t in enumerate(times):
            decay = jnp.exp(-rates * t)
            near.append(jnp.sum(weights * decay, axis=0, keepdims=True))
            far.append(jnp.sum(far_weights * decay, axis=0, keepdims=True))
            decay_ref[j * modes : (j + 1) * modes, c:d] = decay
            spread_ref[j * modes : (j + 1) * modes, c:d] = later * decay
        blank = [jnp.zeros((PADDED - NODES, d - c), jnp.float32)]
        near_ref[:, c:d] = jnp.concatenate(near + blank, axis=0)
        far_ref[:, c:d] = jnp.concatenate(far + blank, axis=0)
        if c < late:
            part = c1[:, c:d] if c < early else c2[:, c - early : d - early]
            state_ref[:, c:d] = modal_state(moment_ref, part, decay_ref, c, d)
            first_ref[:, c:d] = jnp.exp(-rates * float(rows - 1))
            second_ref[:, c:d] = jnp.exp(-rates * float(rows - 2))
    for copy in copies:
        copy.wait()


def modal_state(moment_ref, mixed, decay_ref, c, d):
    halves = jnp.dot(moment_ref[...], mixed, preferred_element_type=jnp.float32)
    moments = halves[:PADDED] + halves[PADDED:]
    modes = decay_ref.shape[0] // NODES
    state = decay_ref[0:modes, c:d] * moments[0:1]
    for j in range(1, NODES):
        state = state + decay_ref[j * modes : (j + 1) * modes, c:d] * moments[j : j + 1]
    return state


def edge_kernel(
    key_ref, value_ref, rims_ref, taps_ref, moment_ref, c1, c2, state_ref, first_ref, second_ref, decay_ref,
    spread_ref, head_ref, middle_ref, *late,
):
    width = key_ref.shape[1]
    early = c1.shape[1] + c2.shape[1]
    modes = state_ref.shape[0]
    keep = (lax.axis_index("seq") >= 1).astype(jnp.float32)
    offset = 0
    for chunk in (c1, c2, *late):
        for a, b in columns(0, chunk.shape[1], 256):
            c, d = offset + a, offset + b
            key_rim = rims_ref[:, width + c : width + d].astype(jnp.float32) * keep
            value_rim = rims_ref[:, 2 * width + c : 2 * width + d].astype(jnp.float32) * keep
            if c < early:
                kf = featurize(key_ref[0:16, c:d].astype(jnp.float32)[:8], taps_ref[1, :, c:d], key_rim)
                vf = featurize(value_ref[0:16, c:d].astype(jnp.float32)[:8], taps_ref[2, :, c:d], value_rim)
                head = (kf * vf).astype(jnp.bfloat16)
                delta = head.astype(jnp.float32) - chunk[0:16, a:b].astype(jnp.float32)[:8]
                state = state_ref[:, c:d] + first_ref[:, c:d] * delta[0:1] + second_ref[:, c:d] * delta[1:2]
            else:
                kf = featurize(key_ref[:, c:d], taps_ref[1, :, c:d], key_rim)
                vf = featurize(value_ref[:, c:d], taps_ref[2, :, c:d], value_rim)
                mixed = (kf * vf).astype(jnp.bfloat16)
                head = mixed[:8]
                state = modal_state(moment_ref, mixed, decay_ref, c, d)
                slot = c - early
                if slot < early and chunk is not late[-1]:
                    second = head_ref[:, slot : slot + b - a].astype(jnp.float32)[1:2]
                    whole = (kf * vf)[:16]
                    row = lax.broadcasted_iota(jnp.int32, whole.shape, 0)
                    chunk[0:16, a:b] = jnp.where(row == 0, second, whole).astype(jnp.bfloat16)
                    chunk[16:, a:b] = mixed[16:]
                else:
                    chunk[:, a:b] = mixed
            head_ref[:, c:d] = head
            middle = [
                jnp.sum(spread_ref[i * modes : (i + 1) * modes, c:d] * state, axis=0, keepdims=True)
                for i in range(NODES)
            ]
            middle.append(jnp.zeros((PADDED - NODES, d - c), jnp.float32))
            middle_ref[:, c:d] = jnp.concatenate(middle, axis=0).astype(middle_ref.dtype)
        offset = offset + chunk.shape[1]


def own_kernel(edge, start, complete, query_ref, head_ref, near_ref, taps_ref, rims_ref, skip_ref, table_ref, *refs):
    *chunks, part_ref, gate_ref, stack_ref = refs
    if complete:
        middle_ref, far_table_ref, *chunks = chunks
    rows, _ = query_ref.shape
    keep = (lax.axis_index("seq") >= 1).astype(jnp.float32)
    offset = start
    for chunk in chunks:
        for a, b in columns(0, chunk.shape[1], stack_ref.shape[1]):
            c, d = offset + a, offset + b
            mixed = chunk[:, a:b].astype(jnp.float32)
            mixed = jnp.concatenate([head_ref[:, c:d].astype(jnp.float32), mixed[8:]], axis=0)
            for j in range(NODES):
                stack_ref[j * rows : (j + 1) * rows, : b - a] = (mixed * near_ref[j : j + 1, c:d]).astype(stack_ref.dtype)
            conv = jnp.dot(table_ref[...], stack_ref[:, : b - a], preferred_element_type=jnp.float32)
            if complete and chunk is chunks[-1]:
                middle = middle_ref[:, c:d].astype(jnp.float32) * keep
                middle = jnp.concatenate([middle, jnp.zeros_like(middle)], axis=0).astype(stack_ref.dtype)
                conv = conv + jnp.dot(far_table_ref[:, NODES * rows :], middle, preferred_element_type=jnp.float32)
            part_ref[:, c - start : d - start] = conv + skip_ref[:, c:d] * mixed
            rim = rims_ref[:, c:d].astype(jnp.float32) * keep
            gate_ref[:, c - start : d - start] = featurize(query_ref[:, c:d], taps_ref[0, :, c:d], rim)
        offset = offset + chunk.shape[1]


def repaired(last, far_ref, pre_ref, right, c, d):
    end = far_ref[0:1, c:d] * last[0]
    for j in range(1, NODES):
        end = end + far_ref[j : j + 1, c:d] * last[j]
    there = (lax.axis_index("seq") >= 2).astype(jnp.float32)
    total = pre_ref[0:16, c:d]
    row = lax.broadcasted_iota(jnp.int32, total.shape, 0)
    total = jnp.where(row == 0, total + end * (right - pre_ref[33:34, c:d] * there), total)
    return pre_ref[16:32, c:d] * total


def send_kernel(start, early, *refs):
    *_, mixed_ref, head_ref, far_ref, table_ref, out_ref, stack_ref = refs
    rows, width = mixed_ref.shape
    for a, b in columns(0, width, stack_ref.shape[1]):
        c, d = start + a, start + b
        mixed = mixed_ref[:, a:b].astype(jnp.float32)
        for j in range(NODES):
            stack_ref[j * rows : (j + 1) * rows, : b - a] = (mixed * far_ref[j : j + 1, c:d]).astype(stack_ref.dtype)
        conv = jnp.dot(table_ref[:, : NODES * rows], stack_ref[:, : b - a], preferred_element_type=jnp.float32)
        out_ref[: rows - 16, a:b] = conv[: rows - 16].astype(out_ref.dtype)
        bottom = conv[rows - 16 :]
        slot = c - early
        if slot < early:
            row = lax.broadcasted_iota(jnp.int32, bottom.shape, 0)
            second = head_ref[:, slot : slot + b - a].astype(jnp.float32)[1:2]
            bottom = jnp.where(row == 15, second, bottom)
        out_ref[rows - 16 :, a:b] = bottom.astype(out_ref.dtype)


def last_kernel(offset, base, slot, last, far_ref, part_ref, gate_ref, pre_ref, _, back_ref, out_ref, stage_ref, repair_ref, sems):
    rows, width = back_ref.shape
    copies = []

    def write(source, tall, c, d):
        copies.append(pltpu.make_async_copy(source, out_ref.at[pl.ds(0, tall), pl.ds(c, d - c)], sems.at[len(copies)]))
        copies[-1].start()

    first, stop = slot
    for c, d in columns(first, stop, 512):
        right = back_ref[rows - 16 :, c - first : d - first].astype(jnp.float32)[15:16]
        repair_ref[:, c - first : d - first] = repaired(last, far_ref, pre_ref, right, c, d).astype(repair_ref.dtype)
    if stop > first:
        write(repair_ref.at[:, pl.ds(0, stop - first)], 16, first, stop)
    for a, b in columns(0, width, LAST_TILE):
        c, d = offset + a, offset + b
        back = back_ref[:, a:b].astype(jnp.float32)
        bottom = back[rows - 16 :]
        row = lax.broadcasted_iota(jnp.int32, bottom.shape, 0)
        back = jnp.concatenate([back[: rows - 16], jnp.where(row == 15, 0.0, bottom)], axis=0)
        total = part_ref[:, c - base : d - base] + back
        stage_ref[:, a:b] = (gate_ref[:, c - base : d - base] * total).astype(stage_ref.dtype)
        write(stage_ref.at[:, pl.ds(a, b - a)], rows, c, d)
    for copy in copies:
        copy.wait()


def finish_kernel(offset, base, slots, last, middle_ref, far_ref, part_ref, gate_ref, table_ref, *refs):
    keep = (lax.axis_index("seq") >= 1).astype(jnp.float32)
    there = (lax.axis_index("seq") >= 2).astype(jnp.float32)
    if slots is None:
        _, *backs, out_ref, pre_ref, stack_ref, stage_ref, sems = refs
    else:
        pre_ref, _, *backs, out_ref, stack_ref, stage_ref, repair_ref, sems = refs
    copies = []

    def write(source, rows, c, d):
        copies.append(pltpu.make_async_copy(source, out_ref.at[pl.ds(0, rows), pl.ds(c, d - c)], sems.at[len(copies)]))
        copies[-1].start()

    at = 0
    for back_ref in backs:
        rows, width = back_ref.shape
        for a, b in columns(0, width, stack_ref.shape[1]):
            c, d = offset + at + a, offset + at + b
            back = back_ref[:, a:b].astype(jnp.float32)
            far = far_ref[:, c:d] * there
            for j in range(NODES):
                stack_ref[j * rows : (j + 1) * rows, : b - a] = (back * far[j : j + 1]).astype(stack_ref.dtype)
            middle = middle_ref[:, c:d].astype(jnp.float32) * keep
            middle = jnp.concatenate([middle, jnp.zeros_like(middle)], axis=0)
            stack_ref[NODES * rows : NODES * rows + 2 * PADDED, : b - a] = middle.astype(stack_ref.dtype)
            conv = jnp.dot(table_ref[...], stack_ref[:, : b - a], preferred_element_type=jnp.float32)
            total = part_ref[:, c - base : d - base] + conv
            gate = gate_ref[:, c - base : d - base]
            stage_ref[:, at + a : at + b] = (gate * total).astype(stage_ref.dtype)
            write(stage_ref.at[:, pl.ds(at + a, b - a)], rows, c, d)
            if slots is None:
                pre_ref[0:16, c:d] = total[:16]
                pre_ref[16:32, c:d] = gate[:16]
                pre_ref[32:40, c:d] = back[:8]
        at = at + width
    start = 0
    for (first, stop), back_ref in zip(slots or (), backs):
        for c, d in columns(first, stop, 512):
            right = back_ref[0:16, c - first : d - first].astype(jnp.float32)[0:1]
            fixed = repaired(last, far_ref, pre_ref, right * there, c, d)
            repair_ref[:, start + c - first : start + d - first] = fixed.astype(repair_ref.dtype)
        if stop > first:
            write(repair_ref.at[:, pl.ds(start, stop - first)], 16, first, stop)
        start = start + stop - first
    for copy in copies:
        copy.wait()


def ring(array, by, closed=True):
    length = lax.axis_size("seq")
    return lax.ppermute(
        array, "seq", [(i, (i + by) % length) for i in range(length) if closed or i + by < length]
    )


def shards(query_in, key_in, value_in, short_filter, residue, rate, skip):
    rows, width = query_in.shape
    kinds, count, _ = short_filter.shape
    edge = count - 1
    modes = residue.shape[1]
    times, last, near_table, far_table, moment_table = make_tables(rows)
    near_table, far_table, moment_table = (jnp.asarray(t) for t in (near_table, far_table, moment_table))
    residue_t, rate_t, skip_row = residue.T, rate.T, skip.reshape(1, width)
    unit = width // 32
    cuts = [0, 7 * unit, 15 * unit, 21 * unit, 27 * unit, 32 * unit]
    count_chunks = len(cuts) - 1
    sizes = [cuts[i + 1] - cuts[i] for i in range(count_chunks)]
    bf16, f32 = jnp.bfloat16, jnp.float32
    vmem, hbm, anywhere = (pl.BlockSpec(memory_space=m) for m in (pltpu.VMEM, pltpu.HBM, pl.ANY))

    def call(body, ins, outs, operands, scratch=(), limit=40, cost=1, **kw):
        return pl.pallas_call(
            body,
            in_specs=ins,
            out_specs=[o[2] if len(o) > 2 else vmem for o in outs],
            out_shape=[jax.ShapeDtypeStruct(o[0], o[1]) for o in outs],
            scratch_shapes=list(scratch),
            compiler_params=pltpu.CompilerParams(vmem_limit_bytes=limit * 1024 * 1024),
            cost_estimate=pl.CostEstimate(flops=cost, bytes_accessed=cost, transcendentals=0),
            **kw,
        )(*(pltpu.with_memory_space_constraint(x, pltpu.HBM) if i is hbm else x for i, x in zip(ins, operands)))

    back = [None] * count_chunks
    (c1,) = call(
        early_kernel,
        [hbm] * 3,
        [((rows, sizes[0]), bf16)],
        (key_in, value_in, short_filter),
        [
            pltpu.VMEM((rows, sizes[0]), bf16),
            pltpu.VMEM((rows, sizes[0]), bf16),
            pltpu.VMEM((kinds, count, sizes[0]), f32),
            pltpu.SemaphoreType.DMA((1 + 2 * len(columns(0, sizes[0], 256)),)),
        ],
    )
    back[0] = ring(c1, 2)
    c2, rims, taps_v, residue_v, rate_v = call(
        functools.partial(second_kernel, cuts[1], edge),
        [anywhere] + [hbm] * 6,
        [
            ((rows, sizes[1]), bf16),
            ((edge, kinds * width), bf16),
            (short_filter.shape, f32),
            ((modes, width), f32),
            ((modes, width), f32),
        ],
        (c1, query_in, key_in, value_in, short_filter, residue_t, rate_t),
        [
            pltpu.VMEM((rows, sizes[1]), bf16),
            pltpu.VMEM((rows, sizes[1]), bf16),
            pltpu.VMEM((kinds, 8, width), bf16),
            pltpu.SemaphoreType.DMA((3 + kinds + 2 * len(columns(0, sizes[1], 256)),)),
        ],
    )
    rims_in = ring(rims, 1)
    back[1] = ring(c2, 2)
    near, far, *states, key_v, value_v = call(
        functools.partial(prepare_kernel, times, rows),
        [hbm] * 2 + [vmem] * 5,
        [((PADDED, width), f32)] * 2
        + [((modes, cuts[2]), f32)] * 3
        + [((NODES * modes, width), f32)] * 2
        + [((rows, width), bf16)] * 2,
        (key_in, value_in, residue_v, rate_v, moment_table, c1, c2),
        [pltpu.SemaphoreType.DMA((4,))],
    )
    late = range(2, count_chunks)
    head, middle, *chunks = call(
        edge_kernel,
        [vmem] * 12,
        [((8, width), bf16), ((PADDED, width), bf16)] + [((rows, sizes[i]), bf16) for i in late],
        (key_v, value_v, rims_in, taps_v, moment_table, c1, c2, *states),
    )
    middle_in = ring(middle, 1)
    for i in late[:-1]:
        back[i] = ring(chunks[i - 2], 2, closed=i < late[-2])

    tile = 512

    def own(first, stop, some, complete):
        return call(
            functools.partial(own_kernel, edge, cuts[first], complete),
            [vmem] * (7 + len(some)),
            [((rows, cuts[stop] - cuts[first]), f32)] * 2,
            (query_in, head, near, taps_v, rims_in, skip_row, near_table, *some),
            [pltpu.VMEM((near_table.shape[1], tile), bf16)],
        )

    early_own = own(0, 2, (c1, c2), False)
    (final,) = call(
        functools.partial(send_kernel, cuts[-2], cuts[2]),
        [anywhere] * 3 + [vmem] * 4,
        [((rows, sizes[-1]), bf16)],
        (middle_in, early_own[0], back[0], chunks[-1], head, far, far_table),
        [pltpu.VMEM((NODES * rows, tile), bf16)],
    )
    back[-1] = ring(final, 2, closed=False)
    late_own = own(2, count_chunks, (middle_in, far_table, *chunks), True)

    def finish(first, stop, out, pre):
        some = range(first, stop)
        size = cuts[stop] - cuts[first]
        pieces = sum(len(columns(0, sizes[i], tile)) for i in some)
        scratch = [pltpu.VMEM((far_table.shape[1], tile), bf16), pltpu.VMEM((rows, size), bf16)]
        slots = None
        if out is not None:
            slots = [(min(cuts[i] - cuts[2], cuts[2]), min(cuts[i + 1] - cuts[2], cuts[2])) for i in some]
            scratch.append(pltpu.VMEM((16, max(sum(b - a for a, b in slots), unit)), bf16))
        scratch.append(pltpu.SemaphoreType.DMA((pieces + len(some),)))
        return call(
            functools.partial(finish_kernel, cuts[first], cuts[0 if out is None else 2], slots, last),
            [vmem] * 5 + ([anywhere] if out is None else [vmem, anywhere]) + [vmem] * len(some),
            [((rows, width), bf16, anywhere)] + ([((40, cuts[2]), f32)] if out is None else []),
            (middle_in, far, *(early_own if out is None else late_own), far_table)
            + ((late_own[0],) if out is None else (pre, out))
            + tuple(back[i] for i in some),
            scratch,
            input_output_aliases={} if out is None else {6: 0},
        )

    out, pre = finish(0, 2, None, None)
    (out,) = finish(2, count_chunks - 1, out, pre)
    slot = (min(cuts[-2] - cuts[2], cuts[2]), min(width - cuts[2], cuts[2]))
    (out,) = call(
        functools.partial(last_kernel, cuts[-2], cuts[2], slot, last),
        [vmem] * 4 + [anywhere, vmem],
        [((rows, width), bf16, anywhere)],
        (far, *late_own, pre, out, back[-1]),
        [
            pltpu.VMEM((rows, sizes[-1]), bf16),
            pltpu.VMEM((16, max(slot[1] - slot[0], unit)), bf16),
            pltpu.SemaphoreType.DMA((len(columns(0, sizes[-1], LAST_TILE)) + 1,)),
        ],
        input_output_aliases={4: 0},
    )
    return out


def solution(mesh):
    return jax.shard_map(
        shards,
        mesh=mesh,
        in_specs=(P(("grp", "seq"), None),) * 3 + (P(),) * 4,
        out_specs=P(("grp", "seq"), None),
        check_vma=False,
    )
```

```python
import functools
import math
from decimal import Decimal, localcontext

import jax
import jax.numpy as jnp
import numpy as np
from jax import lax
from jax.experimental import pallas as pl
from jax.experimental.pallas import tpu as pltpu
from jax.sharding import PartitionSpec as P

RATE_LOW, RATE_HIGH = 0.000390625, 0.03
NODES = 7
PADDED = 8
LAST_TILE = 256


def separable_basis(rows):
    cosines = [math.cos(math.pi * (j + 0.5) / NODES) for j in range(NODES)]
    with localcontext() as context:
        context.prec = 50
        times = [Decimal(str(round((rows - 1) / 2 * (1 - v), 2))) for v in cosines]
        span = RATE_HIGH - RATE_LOW
        rates = [Decimal(str(round(RATE_LOW + span * ((1 - v) / 2) ** 1.3, 6))) for v in cosines]
        table = [
            [(-r * t).exp() for t in times] + [(-r * t).exp() for t in range(rows)] for r in rates
        ]
        for i in range(NODES):
            best = max(range(i, NODES), key=lambda k: abs(table[k][i]))
            table[i], table[best] = table[best], table[i]
            inverse = 1 / table[i][i]
            table[i] = [v * inverse for v in table[i]]
            for k in range(NODES):
                if k != i:
                    factor = table[k][i]
                    table[k] = [a - factor * b for a, b in zip(table[k], table[i])]
        basis = np.array([[float(v) for v in table[i][NODES:]] for i in range(NODES)], np.float64)
    return [float(t) for t in times], basis


def make_tables(rows):
    times, basis = separable_basis(rows)
    place = np.arange(rows)
    delta = place[:, None] - place[None, :]
    wrapped = basis[:, delta % rows]
    lower = np.where(delta[None] >= 0, wrapped, 0.0)
    upper = np.where(delta[None] < 0, wrapped, 0.0)
    near = np.concatenate(list(lower), axis=1).astype(np.float32)
    far = np.concatenate(list(upper) + [basis.T, np.zeros((rows, 2 * PADDED - NODES))], axis=1).astype(np.float32)
    moments = np.zeros((PADDED, rows), np.float32)
    moments[:NODES] = basis[:, ::-1]
    high = moments.astype(jnp.bfloat16)
    low = (moments - high.astype(np.float32)).astype(jnp.bfloat16)
    last = [float(v) for v in basis[:, rows - 1]]
    return times, last, near.astype(jnp.bfloat16), far.astype(jnp.bfloat16), np.concatenate([high, low], axis=0)


def shifted(whole, offset, rim):
    rolled = pltpu.roll(whole, offset, axis=0)
    top = rolled[:8]
    row = lax.broadcasted_iota(jnp.int32, top.shape, 0)
    for r in range(offset):
        at = None if rim is None else rim.shape[0] - offset + r
        top = jnp.where(row == r, 0.0 if rim is None else rim[at : at + 1], top)
    return top if whole.shape[0] == 8 else jnp.concatenate([top, rolled[8:]], axis=0)


def featurize(signal, taps, rim=None):
    whole = signal.astype(jnp.float32)
    result = taps[0:1] * whole
    for offset in range(1, taps.shape[0]):
        result = result + taps[offset : offset + 1] * shifted(whole, offset, rim)
    return result


def columns(start, stop, step):
    return [(at, min(at + step, stop)) for at in range(start, stop, step)]


def early_kernel(key_ref, value_ref, taps_ref, mixed_ref, key_vmem, value_vmem, taps_vmem, sems):
    rows, width = mixed_ref.shape
    spans = columns(0, width, 256)
    taps_copy = pltpu.make_async_copy(taps_ref.at[:, :, pl.ds(0, width)], taps_vmem, sems.at[0])
    taps_copy.start()
    copies = []
    for n, (a, b) in enumerate(spans):
        at = pl.ds(a, b - a)
        pair = (
            pltpu.make_async_copy(key_ref.at[:, at], key_vmem.at[:, at], sems.at[1 + 2 * n]),
            pltpu.make_async_copy(value_ref.at[:, at], value_vmem.at[:, at], sems.at[2 + 2 * n]),
        )
        for copy in pair:
            copy.start()
        copies.append(pair)
    taps_copy.wait()
    for (a, b), pair in zip(spans, copies):
        for copy in pair:
            copy.wait()
        kf = featurize(key_vmem[:, a:b], taps_vmem[1, :, a:b])
        vf = featurize(value_vmem[:, a:b], taps_vmem[2, :, a:b])
        mixed_ref[:, a:b] = (kf * vf).astype(mixed_ref.dtype)


def second_kernel(
    start, edge, _, query_ref, key_ref, value_ref, taps_ref, residue_ref, rate_ref, mixed_ref, rims_ref, taps_vmem,
    residue_vmem, rate_vmem, key_vmem, value_vmem, held, sems,
):
    rows, width = mixed_ref.shape
    whole = key_ref.shape[1]
    count = 0

    def copy(source, target):
        nonlocal count
        made = pltpu.make_async_copy(source, target, sems.at[count])
        made.start()
        count += 1
        return made

    taps_copy = copy(taps_ref, taps_vmem)
    spans = columns(0, width, 256)
    copies = [
        [
            copy(ref.at[:, pl.ds(start + a, b - a)], vmem.at[:, pl.ds(a, b - a)])
            for ref, vmem in ((key_ref, key_vmem), (value_ref, value_vmem))
        ]
        for a, b in spans
    ]
    rest = [copy(ref.at[pl.ds(rows - 8, 8)], held.at[n]) for n, ref in enumerate((query_ref, key_ref, value_ref))]
    rest += [copy(residue_ref, residue_vmem), copy(rate_ref, rate_vmem)]
    taps_copy.wait()
    for (a, b), pair in zip(spans, copies):
        for made in pair:
            made.wait()
        kf = featurize(key_vmem[:, a:b], taps_vmem[1, :, start + a : start + b])
        vf = featurize(value_vmem[:, a:b], taps_vmem[2, :, start + a : start + b])
        mixed_ref[:, a:b] = (kf * vf).astype(mixed_ref.dtype)
    for made in rest:
        made.wait()
    for n in range(held.shape[0]):
        rims_ref[:, n * whole : (n + 1) * whole] = held[n][8 - edge :]


def prepare_kernel(
    times, rows, key_ref, value_ref, residue_ref, rate_ref, moment_ref, c1, c2, near_ref, far_ref, state_ref, first_ref,
    second_ref, decay_ref, spread_ref, key_vmem, value_vmem, sems,
):
    modes, width = rate_ref.shape
    early, late = c1.shape[1], state_ref.shape[1]
    copies = []
    for ref, vmem in ((key_ref, key_vmem), (value_ref, value_vmem)):
        for tall, a, b in ((rows, late, width), (16, 0, late)):
            at = (pl.ds(0, tall), pl.ds(a, b - a))
            copies.append(pltpu.make_async_copy(ref.at[at], vmem.at[at], sems.at[len(copies)]))
            copies[-1].start()
    for c, d in columns(0, early, 256) + columns(early, late, 256) + columns(late, width, 256):
        weights, rates = residue_ref[:, c:d], rate_ref[:, c:d]
        far_weights = weights * jnp.exp(-rates * float(rows))
        later = weights * jnp.exp(-rates)
        near, far = [], []
        for j, t in enumerate(times):
            decay = jnp.exp(-rates * t)
            near.append(jnp.sum(weights * decay, axis=0, keepdims=True))
            far.append(jnp.sum(far_weights * decay, axis=0, keepdims=True))
            decay_ref[j * modes : (j + 1) * modes, c:d] = decay
            spread_ref[j * modes : (j + 1) * modes, c:d] = later * decay
        blank = [jnp.zeros((PADDED - NODES, d - c), jnp.float32)]
        near_ref[:, c:d] = jnp.concatenate(near + blank, axis=0)
        far_ref[:, c:d] = jnp.concatenate(far + blank, axis=0)
        if c < late:
            part = c1[:, c:d] if c < early else c2[:, c - early : d - early]
            state_ref[:, c:d] = modal_state(moment_ref, part, decay_ref, c, d)
            first_ref[:, c:d] = jnp.exp(-rates * float(rows - 1))
            second_ref[:, c:d] = jnp.exp(-rates * float(rows - 2))
    for copy in copies:
        copy.wait()


def modal_state(moment_ref, mixed, decay_ref, c, d):
    halves = jnp.dot(moment_ref[...], mixed, preferred_element_type=jnp.float32)
    moments = halves[:PADDED] + halves[PADDED:]
    modes = decay_ref.shape[0] // NODES
    state = decay_ref[0:modes, c:d] * moments[0:1]
    for j in range(1, NODES):
        state = state + decay_ref[j * modes : (j + 1) * modes, c:d] * moments[j : j + 1]
    return state


def edge_kernel(
    key_ref, value_ref, rims_ref, taps_ref, moment_ref, c1, c2, state_ref, first_ref, second_ref, decay_ref,
    spread_ref, head_ref, middle_ref, *late,
):
    *late, odd_ref = late
    width = key_ref.shape[1]
    early = c1.shape[1] + c2.shape[1]
    modes = state_ref.shape[0]
    keep = (lax.axis_index("seq") >= 1).astype(jnp.float32)
    offset = 0
    for chunk in (c1, c2, *late):
        for a, b in columns(0, chunk.shape[1], 256):
            c, d = offset + a, offset + b
            key_rim = rims_ref[:, width + c : width + d].astype(jnp.float32) * keep
            value_rim = rims_ref[:, 2 * width + c : 2 * width + d].astype(jnp.float32) * keep
            if c < early:
                kf = featurize(key_ref[0:16, c:d].astype(jnp.float32)[:8], taps_ref[1, :, c:d], key_rim)
                vf = featurize(value_ref[0:16, c:d].astype(jnp.float32)[:8], taps_ref[2, :, c:d], value_rim)
                head = (kf * vf).astype(jnp.bfloat16)
                delta = head.astype(jnp.float32) - chunk[0:16, a:b].astype(jnp.float32)[:8]
                state = state_ref[:, c:d] + first_ref[:, c:d] * delta[0:1] + second_ref[:, c:d] * delta[1:2]
            else:
                kf = featurize(key_ref[:, c:d], taps_ref[1, :, c:d], key_rim)
                vf = featurize(value_ref[:, c:d], taps_ref[2, :, c:d], value_rim)
                mixed = (kf * vf).astype(jnp.bfloat16)
                head = mixed[:8]
                state = modal_state(moment_ref, mixed, decay_ref, c, d)
                slot = c - early
                if slot < early and chunk is not late[-1]:
                    second = head_ref[:, slot : slot + b - a].astype(jnp.float32)[1:2]
                    whole = (kf * vf)[:16]
                    row = lax.broadcasted_iota(jnp.int32, whole.shape, 0)
                    chunk[0:16, a:b] = jnp.where(row == 0, second, whole).astype(jnp.bfloat16)
                    chunk[16:, a:b] = mixed[16:]
                else:
                    chunk[:, a:b] = mixed
            head_ref[:, c:d] = head
            middle = [
                jnp.sum(spread_ref[i * modes : (i + 1) * modes, c:d] * state, axis=0, keepdims=True)
                for i in range(NODES)
            ]
            for i in range(0, NODES - 1, 2):
                pair = jnp.concatenate(middle[i : i + 2], axis=0)
                middle_ref[:, i // 2 * width + c : i // 2 * width + d] = pair.astype(middle_ref.dtype)
            odd_ref[0:1, c:d] = middle[-1]
        offset = offset + chunk.shape[1]
    half = width // 2
    pair = jnp.concatenate([odd_ref[0:1, :half], odd_ref[0:1, half:]], axis=0)
    middle_ref[:, NODES // 2 * width :] = pair.astype(middle_ref.dtype)


def middle_rows(middle_ref, c, d):
    width = middle_ref.shape[1] * 2 // NODES
    half, base = width // 2, NODES // 2 * width
    parts = [middle_ref[:, i * width + c : i * width + d].astype(jnp.float32) for i in range(NODES // 2)]
    odd = []
    if c < half:
        odd.append(middle_ref[:, base + c : base + min(d, half)].astype(jnp.float32)[0:1])
    if d > half:
        odd.append(middle_ref[:, base + max(c, half) - half : base + d - half].astype(jnp.float32)[1:2])
    parts.append(odd[0] if len(odd) == 1 else jnp.concatenate(odd, axis=1))
    parts.append(jnp.zeros((2 * PADDED - NODES, d - c), jnp.float32))
    return jnp.concatenate(parts, axis=0)


def own_kernel(edge, start, complete, query_ref, head_ref, near_ref, taps_ref, rims_ref, skip_ref, table_ref, *refs):
    *chunks, part_ref, gate_ref, stack_ref = refs
    if complete:
        middle_ref, far_table_ref, *chunks = chunks
    rows, _ = query_ref.shape
    keep = (lax.axis_index("seq") >= 1).astype(jnp.float32)
    offset = start
    for chunk in chunks:
        for a, b in columns(0, chunk.shape[1], stack_ref.shape[1]):
            c, d = offset + a, offset + b
            mixed = chunk[:, a:b].astype(jnp.float32)
            mixed = jnp.concatenate([head_ref[:, c:d].astype(jnp.float32), mixed[8:]], axis=0)
            for j in range(NODES):
                stack_ref[j * rows : (j + 1) * rows, : b - a] = (mixed * near_ref[j : j + 1, c:d]).astype(stack_ref.dtype)
            conv = jnp.dot(table_ref[...], stack_ref[:, : b - a], preferred_element_type=jnp.float32)
            if complete and chunk is chunks[-1]:
                middle = (middle_rows(middle_ref, c, d) * keep).astype(stack_ref.dtype)
                conv = conv + jnp.dot(far_table_ref[:, NODES * rows :], middle, preferred_element_type=jnp.float32)
            part_ref[:, c - start : d - start] = conv + skip_ref[:, c:d] * mixed
            rim = rims_ref[:, c:d].astype(jnp.float32) * keep
            gate_ref[:, c - start : d - start] = featurize(query_ref[:, c:d], taps_ref[0, :, c:d], rim)
        offset = offset + chunk.shape[1]


def repaired(last, far_ref, pre_ref, right, c, d):
    end = far_ref[0:1, c:d] * last[0]
    for j in range(1, NODES):
        end = end + far_ref[j : j + 1, c:d] * last[j]
    there = (lax.axis_index("seq") >= 2).astype(jnp.float32)
    total = pre_ref[0:16, c:d]
    row = lax.broadcasted_iota(jnp.int32, total.shape, 0)
    total = jnp.where(row == 0, total + end * (right - pre_ref[33:34, c:d] * there), total)
    return pre_ref[16:32, c:d] * total


def send_kernel(start, early, *refs):
    *_, mixed_ref, head_ref, far_ref, table_ref, out_ref, stack_ref = refs
    rows, width = mixed_ref.shape
    for a, b in columns(0, width, stack_ref.shape[1]):
        c, d = start + a, start + b
        mixed = mixed_ref[:, a:b].astype(jnp.float32)
        for j in range(NODES):
            stack_ref[j * rows : (j + 1) * rows, : b - a] = (mixed * far_ref[j : j + 1, c:d]).astype(stack_ref.dtype)
        conv = jnp.dot(table_ref[:, : NODES * rows], stack_ref[:, : b - a], preferred_element_type=jnp.float32)
        out_ref[: rows - 16, a:b] = conv[: rows - 16].astype(out_ref.dtype)
        bottom = conv[rows - 16 :]
        slot = c - early
        if slot < early:
            row = lax.broadcasted_iota(jnp.int32, bottom.shape, 0)
            second = head_ref[:, slot : slot + b - a].astype(jnp.float32)[1:2]
            bottom = jnp.where(row == 15, second, bottom)
        out_ref[rows - 16 :, a:b] = bottom.astype(out_ref.dtype)


def last_kernel(offset, base, slot, last, far_ref, part_ref, gate_ref, pre_ref, _, back_ref, out_ref, stage_ref, repair_ref, sems):
    rows, width = back_ref.shape
    copies = []

    def write(source, tall, c, d):
        copies.append(pltpu.make_async_copy(source, out_ref.at[pl.ds(0, tall), pl.ds(c, d - c)], sems.at[len(copies)]))
        copies[-1].start()

    first, stop = slot
    for c, d in columns(first, stop, 512):
        right = back_ref[rows - 16 :, c - first : d - first].astype(jnp.float32)[15:16]
        repair_ref[:, c - first : d - first] = repaired(last, far_ref, pre_ref, right, c, d).astype(repair_ref.dtype)
    if stop > first:
        write(repair_ref.at[:, pl.ds(0, stop - first)], 16, first, stop)
    for a, b in columns(0, width, LAST_TILE):
        c, d = offset + a, offset + b
        back = back_ref[:, a:b].astype(jnp.float32)
        bottom = back[rows - 16 :]
        row = lax.broadcasted_iota(jnp.int32, bottom.shape, 0)
        back = jnp.concatenate([back[: rows - 16], jnp.where(row == 15, 0.0, bottom)], axis=0)
        total = part_ref[:, c - base : d - base] + back
        stage_ref[:, a:b] = (gate_ref[:, c - base : d - base] * total).astype(stage_ref.dtype)
        write(stage_ref.at[:, pl.ds(a, b - a)], rows, c, d)
    for copy in copies:
        copy.wait()


def finish_kernel(offset, base, slots, last, middle_ref, far_ref, part_ref, gate_ref, table_ref, *refs):
    keep = (lax.axis_index("seq") >= 1).astype(jnp.float32)
    there = (lax.axis_index("seq") >= 2).astype(jnp.float32)
    if slots is None:
        _, *backs, out_ref, pre_ref, stack_ref, stage_ref, sems = refs
    else:
        pre_ref, _, *backs, out_ref, stack_ref, stage_ref, repair_ref, sems = refs
    copies = []

    def write(source, rows, c, d):
        copies.append(pltpu.make_async_copy(source, out_ref.at[pl.ds(0, rows), pl.ds(c, d - c)], sems.at[len(copies)]))
        copies[-1].start()

    at = 0
    for back_ref in backs:
        rows, width = back_ref.shape
        for a, b in columns(0, width, stack_ref.shape[1]):
            c, d = offset + at + a, offset + at + b
            back = back_ref[:, a:b].astype(jnp.float32)
            far = far_ref[:, c:d] * there
            for j in range(NODES):
                stack_ref[j * rows : (j + 1) * rows, : b - a] = (back * far[j : j + 1]).astype(stack_ref.dtype)
            middle = middle_rows(middle_ref, c, d) * keep
            stack_ref[NODES * rows : NODES * rows + 2 * PADDED, : b - a] = middle.astype(stack_ref.dtype)
            conv = jnp.dot(table_ref[...], stack_ref[:, : b - a], preferred_element_type=jnp.float32)
            total = part_ref[:, c - base : d - base] + conv
            gate = gate_ref[:, c - base : d - base]
            stage_ref[:, at + a : at + b] = (gate * total).astype(stage_ref.dtype)
            write(stage_ref.at[:, pl.ds(at + a, b - a)], rows, c, d)
            if slots is None:
                pre_ref[0:16, c:d] = total[:16]
                pre_ref[16:32, c:d] = gate[:16]
                pre_ref[32:40, c:d] = back[:8]
        at = at + width
    start = 0
    for (first, stop), back_ref in zip(slots or (), backs):
        for c, d in columns(first, stop, 512):
            right = back_ref[0:16, c - first : d - first].astype(jnp.float32)[0:1]
            fixed = repaired(last, far_ref, pre_ref, right * there, c, d)
            repair_ref[:, start + c - first : start + d - first] = fixed.astype(repair_ref.dtype)
        if stop > first:
            write(repair_ref.at[:, pl.ds(start, stop - first)], 16, first, stop)
        start = start + stop - first
    for copy in copies:
        copy.wait()


def ring(array, by, closed=True):
    length = lax.axis_size("seq")
    return lax.ppermute(
        array, "seq", [(i, (i + by) % length) for i in range(length) if closed or i + by < length]
    )


def shards(query_in, key_in, value_in, short_filter, residue, rate, skip):
    rows, width = query_in.shape
    kinds, count, _ = short_filter.shape
    edge = count - 1
    modes = residue.shape[1]
    times, last, near_table, far_table, moment_table = make_tables(rows)
    near_table, far_table, moment_table = (jnp.asarray(t) for t in (near_table, far_table, moment_table))
    residue_t, rate_t, skip_row = residue.T, rate.T, skip.reshape(1, width)
    unit = width // 32
    cuts = [0, 7 * unit, 15 * unit, 21 * unit, 27 * unit, 32 * unit]
    count_chunks = len(cuts) - 1
    sizes = [cuts[i + 1] - cuts[i] for i in range(count_chunks)]
    bf16, f32 = jnp.bfloat16, jnp.float32
    vmem, hbm, anywhere = (pl.BlockSpec(memory_space=m) for m in (pltpu.VMEM, pltpu.HBM, pl.ANY))

    def call(body, ins, outs, operands, scratch=(), limit=40, cost=1, **kw):
        return pl.pallas_call(
            body,
            in_specs=ins,
            out_specs=[o[2] if len(o) > 2 else vmem for o in outs],
            out_shape=[jax.ShapeDtypeStruct(o[0], o[1]) for o in outs],
            scratch_shapes=list(scratch),
            compiler_params=pltpu.CompilerParams(vmem_limit_bytes=limit * 1024 * 1024),
            cost_estimate=pl.CostEstimate(flops=cost, bytes_accessed=cost, transcendentals=0),
            **kw,
        )(*(pltpu.with_memory_space_constraint(x, pltpu.HBM) if i is hbm else x for i, x in zip(ins, operands)))

    back = [None] * count_chunks
    (c1,) = call(
        early_kernel,
        [hbm] * 3,
        [((rows, sizes[0]), bf16)],
        (key_in, value_in, short_filter),
        [
            pltpu.VMEM((rows, sizes[0]), bf16),
            pltpu.VMEM((rows, sizes[0]), bf16),
            pltpu.VMEM((kinds, count, sizes[0]), f32),
            pltpu.SemaphoreType.DMA((1 + 2 * len(columns(0, sizes[0], 256)),)),
        ],
    )
    back[0] = ring(c1, 2)
    c2, rims, taps_v, residue_v, rate_v = call(
        functools.partial(second_kernel, cuts[1], edge),
        [anywhere] + [hbm] * 6,
        [
            ((rows, sizes[1]), bf16),
            ((edge, kinds * width), bf16),
            (short_filter.shape, f32),
            ((modes, width), f32),
            ((modes, width), f32),
        ],
        (c1, query_in, key_in, value_in, short_filter, residue_t, rate_t),
        [
            pltpu.VMEM((rows, sizes[1]), bf16),
            pltpu.VMEM((rows, sizes[1]), bf16),
            pltpu.VMEM((kinds, 8, width), bf16),
            pltpu.SemaphoreType.DMA((3 + kinds + 2 * len(columns(0, sizes[1], 256)),)),
        ],
    )
    rims_in = ring(rims, 1)
    back[1] = ring(c2, 2)
    near, far, *states, key_v, value_v = call(
        functools.partial(prepare_kernel, times, rows),
        [hbm] * 2 + [vmem] * 5,
        [((PADDED, width), f32)] * 2
        + [((modes, cuts[2]), f32)] * 3
        + [((NODES * modes, width), f32)] * 2
        + [((rows, width), bf16)] * 2,
        (key_in, value_in, residue_v, rate_v, moment_table, c1, c2),
        [pltpu.SemaphoreType.DMA((4,))],
    )
    late = range(2, count_chunks)
    head, middle, *chunks = call(
        edge_kernel,
        [vmem] * 12,
        [((8, width), bf16), ((2, NODES * width // 2), bf16)] + [((rows, sizes[i]), bf16) for i in late],
        (key_v, value_v, rims_in, taps_v, moment_table, c1, c2, *states),
        [pltpu.VMEM((8, width), f32)],
    )
    middle_in = ring(middle, 1)
    for i in late[:-1]:
        back[i] = ring(chunks[i - 2], 2, closed=i < late[-2])

    tile = 512

    def own(first, stop, some, complete):
        return call(
            functools.partial(own_kernel, edge, cuts[first], complete),
            [vmem] * (7 + len(some)),
            [((rows, cuts[stop] - cuts[first]), f32)] * 2,
            (query_in, head, near, taps_v, rims_in, skip_row, near_table, *some),
            [pltpu.VMEM((near_table.shape[1], tile), bf16)],
        )

    early_own = own(0, 2, (c1, c2), False)
    (final,) = call(
        functools.partial(send_kernel, cuts[-2], cuts[2]),
        [anywhere] * 3 + [vmem] * 4,
        [((rows, sizes[-1]), bf16)],
        (middle_in, early_own[0], back[0], chunks[-1], head, far, far_table),
        [pltpu.VMEM((NODES * rows, tile), bf16)],
    )
    back[-1] = ring(final, 2, closed=False)
    late_own = own(2, count_chunks, (middle_in, far_table, *chunks), True)

    def finish(first, stop, out, pre):
        some = range(first, stop)
        size = cuts[stop] - cuts[first]
        pieces = sum(len(columns(0, sizes[i], tile)) for i in some)
        scratch = [pltpu.VMEM((far_table.shape[1], tile), bf16), pltpu.VMEM((rows, size), bf16)]
        slots = None
        if out is not None:
            slots = [(min(cuts[i] - cuts[2], cuts[2]), min(cuts[i + 1] - cuts[2], cuts[2])) for i in some]
            scratch.append(pltpu.VMEM((16, max(sum(b - a for a, b in slots), unit)), bf16))
        scratch.append(pltpu.SemaphoreType.DMA((pieces + len(some),)))
        return call(
            functools.partial(finish_kernel, cuts[first], cuts[0 if out is None else 2], slots, last),
            [vmem] * 5 + ([anywhere] if out is None else [vmem, anywhere]) + [vmem] * len(some),
            [((rows, width), bf16, anywhere)] + ([((40, cuts[2]), f32)] if out is None else []),
            (middle_in, far, *(early_own if out is None else late_own), far_table)
            + ((late_own[0],) if out is None else (pre, out))
            + tuple(back[i] for i in some),
            scratch,
            input_output_aliases={} if out is None else {6: 0},
        )

    out, pre = finish(0, 2, None, None)
    (out,) = finish(2, count_chunks - 1, out, pre)
    slot = (min(cuts[-2] - cuts[2], cuts[2]), min(width - cuts[2], cuts[2]))
    (out,) = call(
        functools.partial(last_kernel, cuts[-2], cuts[2], slot, last),
        [vmem] * 4 + [anywhere, vmem],
        [((rows, width), bf16, anywhere)],
        (far, *late_own, pre, out, back[-1]),
        [
            pltpu.VMEM((rows, sizes[-1]), bf16),
            pltpu.VMEM((16, max(slot[1] - slot[0], unit)), bf16),
            pltpu.SemaphoreType.DMA((len(columns(0, sizes[-1], LAST_TILE)) + 1,)),
        ],
        input_output_aliases={4: 0},
    )
    return out


def solution(mesh):
    return jax.shard_map(
        shards,
        mesh=mesh,
        in_specs=(P(("grp", "seq"), None),) * 3 + (P(),) * 4,
        out_specs=P(("grp", "seq"), None),
        check_vma=False,
    )
```
